256 devices in a mesh: lat: 16 (over x_lo, z), lon: 8 (over y, core), section: 2 (over x_hi).
Axes of the slice: x: 4 (x_hi: 2, x_lo: 2; x = x_hi * 2 + x_lo), y: 4, z: 8, core: 2. Of those that a mesh axis runs over, the one named last changes fastest.
Arguments:
- fields: bfloat16 [2, 4, 96, 96, 1024], P(None, None, 'lat', 'lon'), may hold values from -6 to 6
- live_cells: int32 [96, 96], P('lat', 'lon'), may hold values 0 or 1
- norm_gain: bfloat16 [2, 1024], P('section'), may hold values from 0.099609375 to 1.8984375
- q_weight: bfloat16 [2, 1024, 512], P('section'), may hold values from -24 to 24
- k_weight: bfloat16 [2, 1024, 512], P('section'), may hold values from -8 to 8
- v_weight: bfloat16 [2, 1024, 512], P('section'), may hold values from -0.1875 to 0.1875
- o_weight: bfloat16 [2, 512, 1024], P('section'), may hold values from -0.5 to 0.5
- merge_gain: float32 [4096], replicated, may hold values from 0.25 to 1.75
- merge_weight: bfloat16 [4096, 2048], P('lat', 'section'), may hold values from -0.09375 to 0.09375
Outputs:
- merged: bfloat16 [2, 4, 48, 48, 2048], P(None, None, 'lat', 'lon', 'section')
The draws below stay inside these ranges and needn't reach their ends.
All inputs are finite; a program needn't handle non-finite values. No bound on the sum of `live_cells` on one device may be relied on, other than what follows from the above.
Results may differ from the reference program's by a relative error of at most 0.015.
Values may be sent and summed in bfloat16 or wider, within the bound.
A program may use at most 128 MiB of HBM per device.

```python
import math
import jax
import jax.numpy as jnp
from jax import lax

D = 1024
HEADS = 8
HEAD = 64
LEV = 4
WLEV = 2
WLAT = 6
WLON = 12
MICRO = 2
LAT = 96
LON = 96


def shared_part(key):
    return jax.random.normal(key, (2, D, HEADS * HEAD), jnp.float32) / math.sqrt(D)


def draw_q_weight(key, part):
    shared = shared_part(key)
    key = jax.random.fold_in(key, 11)
    private = jax.random.normal(key, shared.shape, jnp.float32) / math.sqrt(D)
    return private.astype(jnp.bfloat16)


def draw_k_weight(key, part):
    shared = shared_part(key)
    key = jax.random.fold_in(key, 23)
    private = jax.random.normal(key, shared.shape, jnp.float32) / math.sqrt(D)
    return private.astype(jnp.bfloat16)


def with_ends(drawn, key, least, high):
    longest = drawn.shape.index(max(drawn.shape))
    spots = []
    for shift in (0, 1):
        where = [jax.random.randint(jax.random.fold_in(key, axis), (), 0, length) for axis, length in enumerate(drawn.shape)]
        where[longest] = (where[longest] + shift) % drawn.shape[longest]
        spots.append(tuple(where))
    return drawn.at[spots[0]].set(least).at[spots[1]].set(high)


def level_of(own_key, dims, pieces, least, largest):
    gain, own = 1.0, jax.random.fold_in(own_key, 6)
    for dim, parts in pieces:
        heights = jnp.exp(jax.random.uniform(jax.random.fold_in(own, dim), (parts,), jnp.float32, least / len(pieces), largest / len(pieces)))
        gain = gain * jnp.repeat(heights, dims[dim] // parts).reshape([-1 if axis == dim else 1 for axis in range(len(dims))])
    return gain


def normal_values(rng, dims, deviation, most, pieces=(), kind=jnp.bfloat16):
    gain = level_of(rng, dims, pieces, -0.22, 0.18) if pieces else 1.0
    drawn = jax.random.normal(rng, dims, jnp.float32) * deviation * gain
    return jnp.minimum(jnp.maximum(drawn, -most), most).astype(kind)


def setup_inputs(seed: int = 0) -> dict:
    streams_of = jax.random.split(jax.random.key(seed), 10)
    fields = normal_values(streams_of[0], (MICRO, LEV, LAT, LON, D), 1.0, 6.0, ((2, 16), (3, 8)))
    live_cells = with_ends((jax.random.randint(streams_of[1], (LAT, LON), 0, 2) < 1).astype(jnp.int32), jax.random.fold_in(streams_of[1], 1), 0, 1)
    norm_gain = jnp.clip(1.0 + 0.18 * jax.random.normal(streams_of[2], (2, D), jnp.float32), 0.099609375, 1.8984375).astype(jnp.bfloat16)
    q_weight = draw_q_weight(jax.random.fold_in(streams_of[9], 71), 0)
    k_weight = draw_k_weight(jax.random.fold_in(streams_of[9], 71), 0)
    v_weight = normal_values(streams_of[5], (2, D, HEADS * HEAD), D ** -0.5, 0.1875, ((0, 2),))
    o_weight = normal_values(streams_of[6], (2, HEADS * HEAD, D), (HEADS * HEAD // 4) ** -0.5, 0.5, ((0, 2),))
    merge_gain = jnp.clip(1.0 + 0.15 * jax.random.normal(streams_of[7], (4 * D,), jnp.float32), 0.25, 1.75)
    merge_weight = normal_values(streams_of[8], (4 * D, 2 * D), (4 * D) ** -0.5, 0.09375, ((0, 16), (1, 2)))
    return dict(fields=fields, live_cells=live_cells, norm_gain=norm_gain, q_weight=q_weight, k_weight=k_weight, v_weight=v_weight, o_weight=o_weight, merge_gain=merge_gain, merge_weight=merge_weight)


def layer_norm(values, gain_row):
    average = lax.optimization_barrier(jnp.mean(values, axis=-1, keepdims=True))
    centred = values - average
    variance = lax.optimization_barrier(jnp.mean(centred * centred, axis=-1, keepdims=True))
    return centred * lax.rsqrt(variance + 1e-05) * gain_row

def window_block(grid_tile, window_ids, live_mask, gain_row, w_query, w_key, w_value, w_out):
    levels, tile_rows, tile_cols, model_width = grid_tile.shape
    head_count = w_query.shape[1] // HEAD
    lat_windows = tile_rows // WLAT
    lon_windows = tile_cols // WLON
    lev_windows = levels // WLEV
    window_size = WLEV * WLAT * WLON
    normed = layer_norm(grid_tile.astype(jnp.float32), gain_row.astype(jnp.float32)).astype(jnp.bfloat16).reshape(-1, model_width)

    def windows(weight):
        projected = jnp.dot(normed, weight, preferred_element_type=jnp.float32).astype(jnp.bfloat16)
        shaped = projected.reshape(lev_windows, WLEV, lat_windows, WLAT, lon_windows, WLON, head_count, HEAD)
        shaped = shaped.transpose(0, 2, 4, 1, 3, 5, 6, 7)
        return shaped.reshape(lev_windows, lat_windows, lon_windows, window_size, head_count, HEAD).astype(jnp.float32)
    queries = windows(w_query)
    keys_win = windows(w_key)
    values_win = windows(w_value)
    token_ids = jnp.broadcast_to(window_ids.reshape(lat_windows, 1, 1, WLAT, 1), (lat_windows, lon_windows, WLEV, WLAT, WLON))
    token_ids = token_ids.reshape(lat_windows, lon_windows, window_size)
    key_live = live_mask.reshape(lat_windows, WLAT, lon_windows, WLON).transpose(0, 2, 1, 3)
    key_live = jnp.broadcast_to(key_live[:, :, None], (lat_windows, lon_windows, WLEV, WLAT, WLON))
    key_live = key_live.reshape(lat_windows, lon_windows, window_size)
    same_window = token_ids[:, :, :, None] == token_ids[:, :, None, :]
    allowed = same_window & ((key_live[:, :, None, :] == 1) | jnp.eye(window_size, dtype=bool))
    scores = jnp.einsum('mnoqhe,mnokhe->mnohqk', queries, keys_win) / math.sqrt(HEAD)
    scores = jnp.where(allowed[None, :, :, None], scores, -1e+30)
    row_max = lax.optimization_barrier(jnp.max(scores, axis=-1, keepdims=True))
    exp_scores = jnp.exp(scores - row_max)
    weights = (exp_scores / lax.optimization_barrier(jnp.sum(exp_scores, axis=-1, keepdims=True))).astype(jnp.bfloat16)
    attended = jnp.einsum('mnohqk,mnokhe->mnoqhe', weights.astype(jnp.float32), values_win).astype(jnp.bfloat16)
    restored = attended.reshape(lev_windows, lat_windows, lon_windows, WLEV, WLAT, WLON, head_count, HEAD)
    restored = restored.transpose(0, 3, 1, 4, 2, 5, 6, 7).reshape(-1, head_count * HEAD)
    result = grid_tile.reshape(-1, model_width).astype(jnp.float32) + jnp.dot(restored, w_out, preferred_element_type=jnp.float32)
    return result.astype(jnp.bfloat16).reshape(grid_tile.shape)

def merge_grid(grid_tile, gain_row, weight):
    quarters = (grid_tile[:, 0::2, 0::2], grid_tile[:, 1::2, 0::2], grid_tile[:, 0::2, 1::2], grid_tile[:, 1::2, 1::2])
    joined = jnp.concatenate(quarters, axis=-1).astype(jnp.float32)
    normed = layer_norm(joined, gain_row).astype(jnp.bfloat16)
    full_shape = normed.shape
    result = jnp.dot(normed.reshape(-1, full_shape[-1]), weight, preferred_element_type=jnp.float32)
    return result.astype(jnp.bfloat16).reshape(full_shape[:-1] + (weight.shape[1],))

def reference(fields, live_cells, norm_gain, q_weight, k_weight, v_weight, o_weight, merge_gain, merge_weight):
    half_rows = WLAT // 2
    half_cols = WLON // 2
    grid_rows = jnp.arange(LAT, dtype=jnp.int32)
    plain_ids = grid_rows // WLAT
    shifted_ids = jnp.roll((grid_rows + half_rows) // WLAT, -half_rows)
    rolled_live = jnp.roll(live_cells, (-half_rows, -half_cols), (0, 1))
    results = []
    for micro_index in range(MICRO):
        first_out = window_block(fields[micro_index], plain_ids, live_cells, norm_gain[0], q_weight[0], k_weight[0], v_weight[0], o_weight[0])
        rolled = jnp.roll(first_out, (-half_rows, -half_cols), (1, 2))
        second_out = window_block(rolled, shifted_ids, rolled_live, norm_gain[1], q_weight[1], k_weight[1], v_weight[1], o_weight[1])
        second_out = jnp.roll(second_out, (half_rows, half_cols), (1, 2))
        results.append(merge_grid(second_out, merge_gain, merge_weight))
    return jnp.stack(results)
```

```python
import jax
import jax.numpy as jnp
import numpy as np
from jax import lax
from jax.experimental import pallas as pl
from jax.experimental.pallas import tpu as pltpu
from jax.sharding import PartitionSpec as P

MESH = pl.DeviceIdType.MESH
F32 = jnp.float32
BF16 = jnp.bfloat16
QT = 72
QP = 80
NT = 4 * QP
D = 1024
DH = 512


def tables():
    perm = np.zeros((NT, 384), np.float32)
    share = np.zeros((NT, NT), np.float32)
    phase = np.zeros((384, NT), np.float32)
    cols = np.zeros((4, 128, NT), np.float32)
    rows = np.zeros((4, 8, NT), np.float32)
    where = {}
    for q in range(4):
        for t in range(QT):
            lev, r, c = t // 18, 3 * (q // 2) + t % 18 // 6, 6 * (q % 2) + t % 6
            where[lev, r, c] = q * QP + t
            perm[q * QP + t, (lev * 6 + r) * 16 + c] = 1
            cols[q, c, q * QP + t] = 1
            rows[q, r, q * QP + t] = 1
    for (la, ra, _), a in where.items():
        for (lb, rb, _), b in where.items():
            if la // 2 == lb // 2:
                share[a, b] = 2 if ra // 3 == rb // 3 else 1
    share[np.arange(NT), np.arange(NT)] = 3
    for k in range(4):
        for lev in range(4):
            for a in range(3):
                for b in range(6):
                    phase[k * 96 + (lev * 3 + a) * 8 + b, where[lev, 2 * a + k % 2, 2 * b + k // 2]] = 1
    return perm, share, phase, cols, rows


def kernel(
    x_ref, live_ref, ng_ref, q_ref, k_ref, v_ref, o_ref, mg_ref, mw_ref,
    pm_ref, em_ref, sm_ref, cs_ref, rs_ref,
    out_ref,
    xin, xp, sx, xs, x2h, ar, attb, nrm, qkv, wqkv, ow, oo, wm, pm, em, sm, cs, bias, lvown, lvs, jb, nb,
    lsem, asend, arecv, hsend, hrecv, gsend, grecv, lsend, lrecv, osend, orecv, zsend, zrecv, xsend, xrecv,
    ysend, yrecv, csend, crecv,
):
    i = lax.axis_index("lat")
    j = lax.axis_index("lon")
    s = lax.axis_index("section")
    z = lax.rem(i, 8)
    xl = lax.div(i, 8)
    y = lax.div(j, 2)
    c = lax.rem(j, 2)
    first = s == 0
    second = s == 1
    sign = 2 * s - 1

    def dev(di, dj, sec):
        return (lax.rem(i + di + 16, 16), lax.rem(j + dj + 8, 8), sec)

    def zdev(d):
        return (i - z + lax.rem(z + d + 8, 8), j, s)

    xdev = (lax.rem(i + 8, 16), j, s)
    cdev = (i, j + 1 - 2 * c, s)

    def rc(src, dst, send, recv, device):
        return pltpu.make_async_remote_copy(
            src_ref=src, dst_ref=dst, send_sem=send, recv_sem=recv, device_id=device, device_id_type=MESH
        )

    greet = [dev(0, 1, s), dev(0, -1, s), dev(1, 0, s), dev(-1, 0, s), dev(1, 1, s), dev(-1, -1, s)]
    greet += [dev(0, 2, s), dev(0, -2, s), dev(0, 4, s), zdev(1), zdev(-1), xdev]
    other = 1 - s
    greet += [dev(0, 0, other), dev(0, 1, other), dev(0, -1, other), dev(1, 0, other), dev(-1, 0, other)]
    greet += [dev(1, 1, other), dev(-1, -1, other)]
    barrier = pltpu.get_barrier_semaphore()
    for d in greet:
        pl.semaphore_signal(barrier, inc=1, device_id=d, device_id_type=MESH)

    local = {}
    plan = [
        ("x0", x_ref.at[0], xin.at[0]), ("pm", pm_ref, pm), ("x1", x_ref.at[1], xin.at[1]),
        ("q", q_ref, wqkv.at[:, 0:512]), ("k", k_ref, wqkv.at[:, 512:1024]), ("v", v_ref, wqkv.at[:, 1024:1536]),
        ("cs", cs_ref, cs), ("em", em_ref, em), ("o", o_ref, ow), ("mw", mw_ref, wm.at[xl, z]), ("sm", sm_ref, sm),
    ]
    for n, (name, src, dst) in enumerate(plan):
        local[name] = pltpu.make_async_copy(src, dst, lsem.at[n])
        local[name].start()

    pl.semaphore_wait(barrier, len(greet))

    def oat(ref, piece):
        return ref.at[pl.ds(pl.multiple_of(piece * 64, 64), 64)]

    def piece_at(dj):
        return lax.rem(j + dj + 8, 8)

    o_from = (2, -2, 4)
    sends = []

    def launch(make, *args):
        make(*args).start()
        sends.append((make, args))

    def o_cross():
        return rc(oat(o_ref, j), oat(oo, j), osend.at[0], orecv.at[0], dev(0, 0, other))

    def o_side(n):
        return rc(oat(oo, j), oat(oo, j), osend.at[1 + n], orecv.at[1 + n], dev(0, -o_from[n], s))

    def o_core(n):
        p = oat(oo, piece_at(((0,) + o_from)[n]))
        return rc(p, p, osend.at[4 + n], orecv.at[4 + n], cdev)

    launch(o_cross)

    def o_step1():
        o_cross().wait_recv()
        for n in range(3):
            launch(o_side, n)
        launch(o_core, 0)

    def o_step2():
        for n, dj in enumerate(o_from):
            p = oat(oo, piece_at(dj))
            rc(p, p, osend.at[1 + n], orecv.at[1 + n], dev(0, dj, s)).wait_recv()
            launch(o_core, 1 + n)

    def o_step3():
        for n, dj in enumerate((0,) + o_from):
            p = oat(oo, lax.rem(j + 1 - 2 * c + dj + 8, 8))
            rc(p, p, osend.at[4 + n], orecv.at[4 + n], cdev).wait_recv()

    e = lax.rem(y, 2)
    cls = 2 * e + c
    ocls = 2 * (1 - e) + c

    def rowsof(k, half=None):
        if half is None:
            return pl.ds(pl.multiple_of(k * 64, 64), 64)
        return pl.ds(pl.multiple_of(k * 64 + half * 32, 32), 32)

    def zat(d):
        return lax.rem(z + d + 8, 8)

    def lane_of(chain):
        return xl if chain == 0 else 1 - xl

    def hop_src(chain, way, t):
        d = -way * (t - 1)
        if chain == 0 and t == 1:
            return mw_ref.at[rowsof(cls)]
        return wm.at[lane_of(chain), zat(d), rowsof(cls)]

    def hop_copy(chain, way, t):
        w = 0 if way == 1 else 1
        dst = wm.at[lane_of(chain), zat(-way * (t - 1)), rowsof(cls)]
        return rc(hop_src(chain, way, t), dst, zsend.at[chain, w, t - 1], zrecv.at[chain, w, t - 1], zdev(way))

    def hop(chain, way, t):
        launch(hop_copy, chain, way, t)

    def hop_wait(chain, way, t):
        w = 0 if way == 1 else 1
        dst = wm.at[lane_of(chain), zat(-way * t), rowsof(cls)]
        rc(dst, dst, zsend.at[chain, w, t - 1], zrecv.at[chain, w, t - 1], zdev(way)).wait_recv()

    units = (0, -1, -2, -3, 1, 2, 3, 4)

    def block_at(u, rows):
        if u == 0:
            return wm.at[1 - xl, z, rows]
        return wm.at[:, zat(units[u]), rows]

    def side_copy(u, h):
        ref = block_at(u, rowsof(cls, h))
        return rc(ref, ref, ysend.at[u, h], yrecv.at[u, h], dev(0, 2 - 4 * h, s))

    def core_copy(u, n):
        ref = block_at(u, rowsof(ocls if n else cls))
        return rc(ref, ref, csend.at[u, n], crecv.at[u, n], cdev)

    def spread(u):
        for h in range(2):
            launch(side_copy, u, h)
        launch(core_copy, u, 0)

    def spread2(u):
        for h, dy in ((0, -2), (1, 2)):
            ref = block_at(u, rowsof(ocls, h))
            rc(ref, ref, ysend.at[u, h], yrecv.at[u, h], dev(0, dy, s)).wait_recv()
        launch(core_copy, u, 1)

    def spread3(u):
        for n, k in ((0, 2 * e + 1 - c), (1, 2 * (1 - e) + 1 - c)):
            ref = block_at(u, rowsof(k))
            rc(ref, ref, csend.at[u, n], crecv.at[u, n], cdev).wait_recv()

    def pair_copy():
        return rc(mw_ref.at[rowsof(cls)], wm.at[xl, z, rowsof(cls)], xsend.at[0], xrecv.at[0], xdev)

    def w_p0():
        launch(pair_copy)
        hop(0, 1, 1)
        hop(0, -1, 1)

    def w_p1():
        ref = wm.at[1 - xl, z, rowsof(cls)]
        rc(ref, ref, xsend.at[0], xrecv.at[0], xdev).wait_recv()
        hop(1, 1, 1)
        hop(1, -1, 1)
        spread(0)

    def w_a(t):
        for way in (1, -1):
            hop_wait(0, way, t)
            if t < 3 or way == 1:
                hop(0, way, t + 1)

    def w_b(t):
        for way in (1, -1):
            hop_wait(1, way, t)
            if t < 3 or way == -1:
                hop(1, way, t + 1)
        spread(t)
        spread(3 + t)

    def w_last():
        hop_wait(0, 1, 4)
        hop_wait(1, -1, 4)
        spread(7)

    def permute(m):
        local[f"x{m}"].wait()
        for g in range(24):
            xp[pl.ds(g * 16, 12), :] = xin[m, g]
        if m == 0:
            local["pm"].wait()

        def step(n, carry):
            cols = pl.ds(pl.multiple_of(n * 256, 256), 256)
            got = jnp.dot(pm[...], xp[:, cols], preferred_element_type=F32).astype(BF16)
            sx[m, :, cols] = got

            @pl.when(first)
            def _():
                xs[m, :, cols] = got

            @pl.when(second)
            def _():
                xs[m, pl.ds(3 * QP, QP), cols] = got[3 * QP:, :]

            return carry

        lax.fori_loop(0, 4, step, 0)

    def slot(ref, m, q):
        return ref.at[m, pl.ds(q * QP, QP)]

    def halo(m, q, start):
        up, side = 1 - q // 2, 1 - q % 2
        d = dev(-up, -side, s) if start else dev(up, side, s)
        return rc(slot(sx, m, q), slot(xs, m, q), hsend.at[m, q], hrecv.at[m, q], d)

    def live_copy(q):
        up, side = 1 - q // 2, 1 - q % 2
        return rc(lvown, lvs.at[q], lsend.at[q], lrecv.at[q], dev(-up, -side, s))

    def att_copy(m, q):
        up, side = 1 - q // 2, 1 - q % 2
        return rc(slot(attb, m, q), slot(ar, m, q), asend.at[m, q], arecv.at[m, q], dev(sign * up, sign * side, other))

    def home_copy(m, q):
        up, side = 1 - q // 2, 1 - q % 2
        return rc(slot(xs, m, q), slot(x2h, m, q), gsend.at[m, q], grecv.at[m, q], dev(up, side, s))

    def add_projected(m, src, weight, dst):
        def step(n, carry):
            cols = pl.ds(pl.multiple_of(n * 256, 256), 256)
            got = jnp.dot(src[m], weight[:, cols], preferred_element_type=F32)
            dst[m, :, cols] = (xs[m, :, cols].astype(F32) + got).astype(BF16)
            return carry

        lax.fori_loop(0, 4, step, 0)

    def make_bias():
        local["cs"].wait()
        local["em"].wait()
        alive = jnp.zeros((1, NT), F32)
        for q in range(4):
            got = jnp.dot(lvs[q].astype(BF16), cs[q], preferred_element_type=F32)
            alive += jnp.sum(got * rs_ref[q], axis=0, keepdims=True)
        edge = jnp.where(jnp.logical_and(second, i == 15), 1.5, 0.5)

        def step(n, carry):
            rows = pl.ds(pl.multiple_of(n * 80, 80), 80)
            code = em[rows, :].astype(F32)
            ok = jnp.logical_or(jnp.logical_and(code > edge, alive > 0.5), code > 2.5)
            bias[rows, :] = jnp.where(ok, 0.0, -1e30)
            return carry

        lax.fori_loop(0, 4, step, 0)

    def attend(m):
        def ln(n, carry):
            rows = pl.ds(pl.multiple_of(n * 32, 32), 32)
            v = xs[m, rows, :].astype(F32)
            v = v - jnp.mean(v, axis=-1, keepdims=True)
            var = jnp.mean(v * v, axis=-1, keepdims=True)
            nrm[rows, :] = (v * lax.rsqrt(var + 1e-05) * ng_ref[...].astype(F32)).astype(BF16)
            return carry

        lax.fori_loop(0, 10, ln, 0)
        if m == 0:
            for name in "qkv":
                local[name].wait()

        def project(n, carry):
            cols = pl.ds(pl.multiple_of(n * 256, 256), 256)
            got = jnp.dot(nrm[...], wqkv[:, cols], preferred_element_type=F32)
            qkv[:, cols] = (got * jnp.where(n < 2, 0.125, 1.0)).astype(BF16)
            return carry

        lax.fori_loop(0, 6, project, 0)

        low = lax.broadcasted_iota(jnp.int32, (NT, 128), 1) < 64

        def heads(n, carry):
            base = pl.multiple_of(n * 128, 128)
            qp = qkv[:, pl.ds(base, 128)]
            kp = qkv[:, pl.ds(base + 512, 128)]
            vp = qkv[:, pl.ds(base + 1024, 128)]
            outs = []
            for mask in (low, jnp.logical_not(low)):
                qm = jnp.where(mask, qp, jnp.zeros_like(qp))
                sc = lax.dot_general(qm, kp, (((1,), (1,)), ((), ())), preferred_element_type=F32) + bias[...]
                ex = jnp.exp(sc - jnp.max(sc, axis=-1, keepdims=True))
                total = jnp.sum(ex, axis=-1, keepdims=True)
                got = jnp.dot(ex.astype(BF16), vp, preferred_element_type=F32)
                outs.append(got / total)
            attb[m, :, pl.ds(base, 128)] = jnp.where(low, outs[0], outs[1]).astype(BF16)
            return carry

        lax.fori_loop(0, 4, heads, 0)

    def block(m):
        @pl.when(second)
        def _():
            for q in range(3):
                halo(m, q, False).wait_recv()
            for q in range(4):
                att_copy(m, q).wait_recv()
            add_projected(m, ar, oo, xs)

        attend(m)
        for q in range(4):
            launch(att_copy, m, q)
        if m == 0:
            local["o"].wait()
        add_projected(m, attb, ow, xs)

        @pl.when(second)
        def _():
            for q in range(3):
                home_copy(m, q).start()
            x2h[m, pl.ds(3 * QP, QP), :] = xs[m, pl.ds(3 * QP, QP), :]

    def merge(m):
        def gather(k, carry):
            rows = pl.ds(pl.multiple_of(k * 96, 32), 96)
            jb[k] = jnp.dot(sm[rows, :], x2h[m], preferred_element_type=F32)
            return carry

        lax.fori_loop(0, 4, gather, 0)

        def ln(n, carry):
            rows = pl.ds(pl.multiple_of(n * 16, 16), 16)
            parts = [jb[k, rows, :] for k in range(4)]
            mean = sum(jnp.sum(p, axis=-1, keepdims=True) for p in parts) * (1.0 / 4096)
            parts = [p - mean for p in parts]
            var = sum(jnp.sum(p * p, axis=-1, keepdims=True) for p in parts) * (1.0 / 4096)
            scale = lax.rsqrt(var + 1e-05)
            for k in range(4):
                nb[k, rows, :] = (parts[k] * scale * mg_ref[k]).astype(BF16)
            return carry

        lax.fori_loop(0, 6, ln, 0)

        def out(n, carry):
            cols = pl.ds(pl.multiple_of(n * 256, 256), 256)
            acc = jnp.zeros((96, 256), F32)
            for k in range(4):
                w = wm[k // 2, pl.ds(4 * (k % 2), 4), :, cols].reshape(1024, 256)
                acc += jnp.dot(nb[k], w, preferred_element_type=F32)
            for g in range(12):
                out_ref[m, g, :, cols] = acc[g * 8 : g * 8 + 6].astype(BF16)
            return carry

        lax.fori_loop(0, 4, out, 0)

    w_p0()
    xp[...] = jnp.zeros_like(xp)
    lvown[...] = jnp.zeros_like(lvown)
    lvown[0:6, 0:12] = live_ref[...].astype(F32)

    @pl.when(first)
    def _():
        for q in range(3):
            lvs[q] = lvown[...]

    lvs[3] = lvown[...]

    @pl.when(second)
    def _():
        for q in range(3):
            live_copy(q).start()

    for m in range(2):
        permute(m)

        @pl.when(second)
        def _():
            for q in range(3):
                halo(m, q, True).start()

    @pl.when(second)
    def _():
        for q in range(3):
            live_copy(q).wait_recv()

    make_bias()

    def early():
        w_p1()
        o_step1()
        w_a(1)
        o_step2()
        w_b(1)
        o_step3()

    mark = len(sends)

    @pl.when(second)
    def _():
        early()
        w_a(2)
        w_b(2)

    del sends[mark:]
    block(0)
    block(1)

    mark = len(sends)

    @pl.when(first)
    def _():
        early()
        w_a(2)
        w_b(2)

    w_a(3)
    w_b(3)
    w_last()
    for u in range(8):
        spread2(u)
    local["mw"].wait()
    local["sm"].wait()
    for u in range(8):
        spread3(u)

    for m in range(2):
        @pl.when(first)
        def _():
            for q in range(4):
                att_copy(m, q).wait_recv()
            add_projected(m, ar, oo, x2h)

        @pl.when(second)
        def _():
            for q in range(3):
                home_copy(m, q).wait_recv()

        merge(m)

    for make, args in sends:
        make(*args).wait_send()

    @pl.when(second)
    def _():
        for q in range(3):
            live_copy(q).wait_send()
            for m in range(2):
                halo(m, q, True).wait_send()
                home_copy(m, q).wait_send()


def body(fields, live_cells, norm_gain, q_weight, k_weight, v_weight, o_weight, merge_gain, merge_weight):
    perm, share, phase, cols, rows = tables()
    anywhere = pl.BlockSpec(memory_space=pl.ANY)
    vmem = pl.BlockSpec(memory_space=pltpu.VMEM)
    dma = pltpu.SemaphoreType.DMA
    out = pl.pallas_call(
        kernel,
        out_shape=jax.ShapeDtypeStruct((2, 12, 6, 1024), BF16),
        in_specs=[anywhere, vmem, vmem, anywhere, anywhere, anywhere, anywhere, vmem, anywhere]
        + [anywhere] * 4 + [vmem],
        out_specs=vmem,
        scratch_shapes=[
            pltpu.VMEM((2, 24, 12, D), BF16),
            pltpu.VMEM((384, D), BF16),
            pltpu.VMEM((2, NT, D), BF16),
            pltpu.VMEM((2, NT, D), BF16),
            pltpu.VMEM((2, NT, D), BF16),
            pltpu.VMEM((2, NT, DH), BF16),
            pltpu.VMEM((2, NT, DH), BF16),
            pltpu.VMEM((NT, D), BF16),
            pltpu.VMEM((NT, 3 * DH), BF16),
            pltpu.VMEM((D, 3 * DH), BF16),
            pltpu.VMEM((DH, D), BF16),
            pltpu.VMEM((DH, D), BF16),
            pltpu.VMEM((2, 8, 256, D), BF16),
            pltpu.VMEM((NT, 384), BF16),
            pltpu.VMEM((NT, NT), BF16),
            pltpu.VMEM((384, NT), BF16),
            pltpu.VMEM((4, 128, NT), BF16),
            pltpu.VMEM((NT, NT), F32),
            pltpu.VMEM((8, 128), F32),
            pltpu.VMEM((4, 8, 128), F32),
            pltpu.VMEM((4, 96, D), F32),
            pltpu.VMEM((4, 96, D), BF16),
            dma((11,)),
            dma((2, 4)), dma((2, 4)), dma((2, 4)), dma((2, 4)), dma((2, 4)), dma((2, 4)),
            dma((4,)), dma((4,)), dma((8,)), dma((8,)), dma((2, 2, 4)), dma((2, 2, 4)), dma((1,)), dma((1,)),
            dma((8, 2)), dma((8, 2)), dma((8, 2)), dma((8, 2)),
        ],
        compiler_params=pltpu.CompilerParams(
            collective_id=0, has_side_effects=True, vmem_limit_bytes=52 * 2**20
        ),
    )(
        fields.reshape(2, 24, 12, D),
        live_cells,
        norm_gain,
        q_weight[0],
        k_weight[0],
        v_weight[0],
        o_weight[0],
        merge_gain.reshape(4, 1, D),
        merge_weight,
        jnp.asarray(perm, BF16),
        jnp.asarray(share, BF16),
        jnp.asarray(phase, BF16),
        jnp.asarray(cols, BF16),
        jnp.asarray(rows, F32),
    )
    return out.reshape(2, 4, 3, 6, D)


def solution(mesh):
    placed = (
        P(None, None, "lat", "lon", None),
        P("lat", "lon"),
        P("section", None),
        P("section", None, None),
        P("section", None, None),
        P("section", None, None),
        P("section", None, None),
        P(),
        P("lat", "section"),
    )
    return jax.shard_map(
        body, mesh=mesh, in_specs=placed, out_specs=P(None, None, "lat", "lon", "section"), check_vma=False
    )
```

```python
import jax
import jax.numpy as jnp
import numpy as np
from jax import lax
from jax.experimental import pallas as pl
from jax.experimental.pallas import tpu as pltpu
from jax.sharding import PartitionSpec as P

MESH = pl.DeviceIdType.MESH
F32 = jnp.float32
BF16 = jnp.bfloat16
QT = 72
QP = 80
NT = 4 * QP
HP = 40
WT = 4 * HP
D = 1024
DH = 512


def tables():
    perm = np.zeros((NT, 4 * QT), np.float32)
    share = np.zeros((WT, WT), np.float32)
    phase = np.zeros((4 * QP, NT), np.float32)
    cols = np.zeros((4, 128, WT), np.float32)
    rows = np.zeros((4, 8, WT), np.float32)
    where = {}
    for q in range(4):
        for t in range(QT):
            lev, r, c = t // 18, 3 * (q // 2) + t % 18 // 6, 6 * (q % 2) + t % 6
            where[lev, r, c] = q * QP + lev // 2 * HP + t % 36
            perm[where[lev, r, c], (r * 12 + c) * 4 + lev] = 1
            cols[q, c, q * HP + t % 36] = 1
            rows[q, r, q * HP + t % 36] = 1
    for a in range(WT):
        for b in range(WT):
            if a % HP < 36 and b % HP < 36:
                share[a, b] = 2 if a // (2 * HP) == b // (2 * HP) else 1
    share[np.arange(WT), np.arange(WT)] = 3
    for k in range(4):
        for lev in range(4):
            for a in range(3):
                for b in range(6):
                    phase[k * QP + (a * 6 + b) * 4 + lev, where[lev, 2 * a + k % 2, 2 * b + k // 2]] = 1
    return perm, share, phase, cols, rows


def kernel(
    x_ref, live_ref, ng_ref, q_ref, k_ref, v_ref, o_ref, mg_ref, mw_ref,
    pm_ref, em_ref, sm_ref, cs_ref, rs_ref,
    out_ref,
    xin, xp, sx, xs, x2h, ar, attb, nrm, qkv, wqkv, ow, oo, wm, pm, em, sm, cs, bias, lvown, lvs, jb, nb,
    lsem, asend, arecv, hsend, hrecv, gsend, grecv, lsend, lrecv, osend, orecv, zsend, zrecv, xsend, xrecv,
    ysend, yrecv, csend, crecv,
):
    i = lax.axis_index("lat")
    j = lax.axis_index("lon")
    s = lax.axis_index("section")
    z = lax.rem(i, 8)
    xl = lax.div(i, 8)
    y = lax.div(j, 2)
    c = lax.rem(j, 2)
    first = s == 0
    second = s == 1
    sign = 2 * s - 1

    def dev(di, dj, sec):
        return (lax.rem(i + di + 16, 16), lax.rem(j + dj + 8, 8), sec)

    def zdev(d):
        return (i - z + lax.rem(z + d + 8, 8), j, s)

    xdev = (lax.rem(i + 8, 16), j, s)
    cdev = (i, j + 1 - 2 * c, s)

    def rc(src, dst, send, recv, device):
        return pltpu.make_async_remote_copy(
            src_ref=src, dst_ref=dst, send_sem=send, recv_sem=recv, device_id=device, device_id_type=MESH
        )

    greet = [dev(0, 1, s), dev(0, -1, s), dev(1, 0, s), dev(-1, 0, s), dev(1, 1, s), dev(-1, -1, s)]
    greet += [dev(0, 2, s), dev(0, -2, s), dev(0, 4, s), zdev(1), zdev(-1), xdev]
    other = 1 - s
    greet += [dev(0, 0, other), dev(0, 1, other), dev(0, -1, other), dev(1, 0, other), dev(-1, 0, other)]
    greet += [dev(1, 1, other), dev(-1, -1, other)]
    barrier = pltpu.get_barrier_semaphore()
    for d in greet:
        pl.semaphore_signal(barrier, inc=1, device_id=d, device_id_type=MESH)

    local = {}
    plan = [
        ("x0", x_ref.at[0], xin.at[0]), ("pm", pm_ref, pm), ("x1", x_ref.at[1], xin.at[1]),
        ("cs", cs_ref, cs), ("em", em_ref, em),
        ("q", q_ref, wqkv.at[:, 0:512]), ("k", k_ref, wqkv.at[:, 512:1024]), ("v", v_ref, wqkv.at[:, 1024:1536]),
        ("o", o_ref, ow), ("mw", mw_ref, wm.at[xl, z]), ("sm", sm_ref, sm),
    ]
    for n, (name, src, dst) in enumerate(plan):
        local[name] = pltpu.make_async_copy(src, dst, lsem.at[n])
        local[name].start()

    pl.semaphore_wait(barrier, len(greet))

    def oat(ref, piece):
        return ref.at[pl.ds(pl.multiple_of(piece * 64, 64), 64)]

    def piece_at(dj):
        return lax.rem(j + dj + 8, 8)

    o_from = (2, -2, 4)
    sends = []

    def launch(make, *args):
        make(*args).start()
        sends.append((make, args))

    def o_cross():
        return rc(oat(o_ref, j), oat(oo, j), osend.at[0], orecv.at[0], dev(0, 0, other))

    def o_side(n):
        return rc(oat(oo, j), oat(oo, j), osend.at[1 + n], orecv.at[1 + n], dev(0, -o_from[n], s))

    def o_core(n):
        p = oat(oo, piece_at(((0,) + o_from)[n]))
        return rc(p, p, osend.at[4 + n], orecv.at[4 + n], cdev)

    launch(o_cross)

    def o_step1():
        o_cross().wait_recv()
        for n in range(3):
            launch(o_side, n)
        launch(o_core, 0)

    def o_step2():
        for n, dj in enumerate(o_from):
            p = oat(oo, piece_at(dj))
            rc(p, p, osend.at[1 + n], orecv.at[1 + n], dev(0, dj, s)).wait_recv()
            launch(o_core, 1 + n)

    def o_step3():
        for n, dj in enumerate((0,) + o_from):
            p = oat(oo, lax.rem(j + 1 - 2 * c + dj + 8, 8))
            rc(p, p, osend.at[4 + n], orecv.at[4 + n], cdev).wait_recv()

    e = lax.rem(y, 2)
    cls = 2 * e + c
    ocls = 2 * (1 - e) + c

    def rowsof(k, half=None):
        if half is None:
            return pl.ds(pl.multiple_of(k * 64, 64), 64)
        return pl.ds(pl.multiple_of(k * 64 + half * 32, 32), 32)

    def zat(d):
        return lax.rem(z + d + 8, 8)

    def lane_of(chain):
        return xl if chain == 0 else 1 - xl

    def hop_src(chain, way, t):
        d = -way * (t - 1)
        if chain == 0 and t == 1:
            return mw_ref.at[rowsof(cls)]
        return wm.at[lane_of(chain), zat(d), rowsof(cls)]

    def hop_copy(chain, way, t):
        w = 0 if way == 1 else 1
        dst = wm.at[lane_of(chain), zat(-way * (t - 1)), rowsof(cls)]
        return rc(hop_src(chain, way, t), dst, zsend.at[chain, w, t - 1], zrecv.at[chain, w, t - 1], zdev(way))

    def hop(chain, way, t):
        launch(hop_copy, chain, way, t)

    def hop_wait(chain, way, t):
        w = 0 if way == 1 else 1
        dst = wm.at[lane_of(chain), zat(-way * t), rowsof(cls)]
        rc(dst, dst, zsend.at[chain, w, t - 1], zrecv.at[chain, w, t - 1], zdev(way)).wait_recv()

    units = (0, -1, -2, -3, 1, 2, 3, 4)

    def block_at(u, rows):
        if u == 0:
            return wm.at[1 - xl, z, rows]
        return wm.at[:, zat(units[u]), rows]

    def side_copy(u, h):
        ref = block_at(u, rowsof(cls, h))
        return rc(ref, ref, ysend.at[u, h], yrecv.at[u, h], dev(0, 2 - 4 * h, s))

    def core_copy(u, n):
        ref = block_at(u, rowsof(ocls if n else cls))
        return rc(ref, ref, csend.at[u, n], crecv.at[u, n], cdev)

    def spread(u):
        for h in range(2):
            launch(side_copy, u, h)
        launch(core_copy, u, 0)

    def spread2(u):
        for h, dy in ((0, -2), (1, 2)):
            ref = block_at(u, rowsof(ocls, h))
            rc(ref, ref, ysend.at[u, h], yrecv.at[u, h], dev(0, dy, s)).wait_recv()
        launch(core_copy, u, 1)

    def spread3(u):
        for n, k in ((0, 2 * e + 1 - c), (1, 2 * (1 - e) + 1 - c)):
            ref = block_at(u, rowsof(k))
            rc(ref, ref, csend.at[u, n], crecv.at[u, n], cdev).wait_recv()

    def pair_copy():
        return rc(mw_ref.at[rowsof(cls)], wm.at[xl, z, rowsof(cls)], xsend.at[0], xrecv.at[0], xdev)

    def w_p0():
        launch(pair_copy)
        hop(0, 1, 1)
        hop(0, -1, 1)

    def w_p1():
        ref = wm.at[1 - xl, z, rowsof(cls)]
        rc(ref, ref, xsend.at[0], xrecv.at[0], xdev).wait_recv()
        hop(1, 1, 1)
        hop(1, -1, 1)
        spread(0)

    def w_a(t):
        for way in (1, -1):
            hop_wait(0, way, t)
            if t < 3 or way == 1:
                hop(0, way, t + 1)

    def w_b(t):
        for way in (1, -1):
            hop_wait(1, way, t)
            if t < 3 or way == -1:
                hop(1, way, t + 1)
        spread(t)
        spread(3 + t)

    def w_last():
        hop_wait(0, 1, 4)
        hop_wait(1, -1, 4)
        spread(7)

    def off(m, q):
        return (1 - q // 2, 1 - q % 2) if m == 0 else (-(q // 2), -(q % 2))

    own = (3, 0)
    away = ((0, 1, 2), (1, 2, 3))

    def permute(m):
        local[f"x{m}"].wait()
        for g in range(QT):
            xp[pl.ds(g * 4, 4), :] = xin[m, g]
        if m == 0:
            local["pm"].wait()

        def step(n, carry):
            cols = pl.ds(pl.multiple_of(n * 256, 256), 256)
            got = jnp.dot(pm[...], xp[:, cols], preferred_element_type=F32).astype(BF16)
            sx[m, :, cols] = got

            @pl.when(first)
            def _():
                xs[m, :, cols] = got

            @pl.when(second)
            def _():
                xs[m, pl.ds(own[m] * QP, QP), cols] = got[own[m] * QP : own[m] * QP + QP, :]

            return carry

        lax.fori_loop(0, 4, step, 0)

    def slot(ref, m, q):
        return ref.at[m, pl.ds(q * QP, QP)]

    def halo(m, q, start):
        up, side = off(m, q)
        d = dev(-up, -side, s) if start else dev(up, side, s)
        return rc(slot(sx, m, q), slot(xs, m, q), hsend.at[m, q], hrecv.at[m, q], d)

    def live_copy(m, q):
        up, side = off(m, q)
        return rc(lvown, lvs.at[m, q], lsend.at[m, q], lrecv.at[m, q], dev(-up, -side, s))

    def att_copy(m, q):
        up, side = off(m, q)
        return rc(slot(attb, m, q), slot(ar, m, q), asend.at[m, q], arecv.at[m, q], dev(sign * up, sign * side, other))

    def home_copy(m, q):
        up, side = off(m, q)
        return rc(slot(xs, m, q), slot(x2h, m, q), gsend.at[m, q], grecv.at[m, q], dev(up, side, s))

    def add_projected(m, src, weight, dst):
        def step(n, carry):
            cols = pl.ds(pl.multiple_of(n * 256, 256), 256)
            got = jnp.dot(src[m], weight[:, cols], preferred_element_type=F32)
            dst[m, :, cols] = (xs[m, :, cols].astype(F32) + got).astype(BF16)
            return carry

        lax.fori_loop(0, 4, step, 0)

    def make_bias(m):
        alive = jnp.zeros((1, WT), F32)
        for q in range(4):
            got = jnp.dot(lvs[m, q].astype(BF16), cs[q], preferred_element_type=F32)
            alive += jnp.sum(got * rs_ref[q], axis=0, keepdims=True)
        cut = jnp.where(jnp.logical_and(second, i == (15 if m == 0 else 0)), 1.5, 0.5)
        code = em[...].astype(F32)
        ok = jnp.logical_or(jnp.logical_and(code > cut, alive > 0.5), code > 2.5)
        bias[m] = jnp.where(ok, 0.0, -1e30)

    def attend(m, hook):
        gain = ng_ref[...].astype(F32)
        for n in range(8):
            v = xs[m, n * HP : n * HP + HP, :].astype(F32)
            v = v - jnp.mean(v, axis=-1, keepdims=True)
            var = jnp.mean(v * v, axis=-1, keepdims=True)
            row = n % 2 * WT + n // 2 * HP
            nrm[row : row + HP, :] = (v * lax.rsqrt(var + 1e-05) * gain).astype(BF16)
        if m == 0:
            for name in "qkv":
                local[name].wait()

        def project(n, carry):
            cols = pl.ds(pl.multiple_of(n * 512, 512), 512)
            got = jnp.dot(nrm[...], wqkv[:, cols], preferred_element_type=F32)
            qkv[:, cols] = (got * jnp.where(n < 1, 0.125, 1.0)).astype(BF16)
            return carry

        lax.fori_loop(0, 3, project, 0)
        hook()
        low = lax.broadcasted_iota(jnp.int32, (WT, 128), 1) < 64
        bm = m * s

        def heads(n, carry):
            base = pl.multiple_of(n * 128, 128)
            for w in range(2):
                rows = pl.ds(w * WT, WT)
                qp = qkv[rows, pl.ds(base, 128)]
                kp = qkv[rows, pl.ds(base + 512, 128)]
                vp = qkv[rows, pl.ds(base + 1024, 128)]
                outs = []
                for mask in (low, jnp.logical_not(low)):
                    qm = jnp.where(mask, qp, jnp.zeros_like(qp))
                    sc = lax.dot_general(qm, kp, (((1,), (1,)), ((), ())), preferred_element_type=F32) + bias[bm]
                    ex = jnp.exp(sc - jnp.max(sc, axis=-1, keepdims=True))
                    total = jnp.sum(ex, axis=-1, keepdims=True)
                    got = jnp.dot(ex.astype(BF16), vp, preferred_element_type=F32)
                    outs.append(got / total)
                both = jnp.where(low, outs[0], outs[1]).astype(BF16)
                for q in range(4):
                    attb[m, pl.ds(q * QP + w * HP, HP), pl.ds(base, 128)] = both[q * HP : q * HP + HP, :]
            return carry

        lax.fori_loop(0, 4, heads, 0)

    def block(m, middle, after):
        @pl.when(second)
        def _():
            for q in away[m]:
                halo(m, q, False).wait_recv()
            for q in range(4):
                att_copy(m, q).wait_recv()
            add_projected(m, ar, oo, xs)

        attend(m, middle)
        for q in range(4):
            launch(att_copy, m, q)
        after()
        if m == 0:
            local["o"].wait()
        add_projected(m, attb, ow, xs)

        @pl.when(second)
        def _():
            for q in away[m]:
                home_copy(m, q).start()
            x2h[m, pl.ds(own[m] * QP, QP), :] = xs[m, pl.ds(own[m] * QP, QP), :]

    def merge(m):
        def gather(k, carry):
            rows = pl.ds(pl.multiple_of(k * QP, QP), QP)
            jb[k] = jnp.dot(sm[rows, :], x2h[m], preferred_element_type=F32)
            return carry

        lax.fori_loop(0, 4, gather, 0)

        def ln(n, carry):
            rows = pl.ds(pl.multiple_of(n * 16, 16), 16)
            parts = [jb[k, rows, :] for k in range(4)]
            mean = sum(jnp.sum(p, axis=-1, keepdims=True) for p in parts) * (1.0 / 4096)
            parts = [p - mean for p in parts]
            var = sum(jnp.sum(p * p, axis=-1, keepdims=True) for p in parts) * (1.0 / 4096)
            scale = lax.rsqrt(var + 1e-05)
            for k in range(4):
                nb[k, rows, :] = (parts[k] * scale * mg_ref[k]).astype(BF16)
            return carry

        lax.fori_loop(0, 5, ln, 0)

        def out(n, carry):
            cols = pl.ds(pl.multiple_of(n * 256, 256), 256)
            acc = jnp.zeros((QP, 256), F32)
            for k in range(4):
                w = wm[k // 2, pl.ds(4 * (k % 2), 4), :, cols].reshape(1024, 256)
                acc += jnp.dot(nb[k], w, preferred_element_type=F32)
            for g in range(18):
                out_ref[m, g, :, cols] = acc[g * 4 : g * 4 + 4].astype(BF16)
            return carry

        lax.fori_loop(0, 4, out, 0)

    lvown[...] = jnp.zeros_like(lvown)
    lvown[0:6, 0:12] = live_ref[...].astype(F32)

    @pl.when(first)
    def _():
        w_p0()
        for m in range(2):
            for q in away[m]:
                lvs[m, q] = lvown[...]

    for m in range(2):
        lvs[m, own[m]] = lvown[...]

    @pl.when(second)
    def _():
        for m in range(2):
            for q in away[m]:
                live_copy(m, q).start()

    permute(0)

    @pl.when(second)
    def _():
        for q in away[0]:
            halo(0, q, True).start()
        permute(1)
        for q in away[1]:
            halo(1, q, True).start()
        w_p0()
        for m in range(2):
            for q in away[m]:
                live_copy(m, q).wait_recv()

    del sends[1:]
    local["cs"].wait()
    local["em"].wait()
    make_bias(0)

    def only(which, *steps):
        def run():
            mark = len(sends)

            @pl.when(which)
            def _():
                for f, *args in steps:
                    f(*args)

            pending.extend(sends[mark:])
            del sends[mark:]

        return run

    pending = []

    def remake():
        sends.append((pair_copy, ()))
        for way in (1, -1):
            for chain in range(2):
                for n in range(1, 5 if way == 1 - 2 * chain else 4):
                    sends.append((hop_copy, (chain, way, n)))
        for n in range(3):
            sends.append((o_side, (n,)))
        for n in range(4):
            sends.append((o_core, (n,)))
        for u in range(7):
            for h in range(2):
                sends.append((side_copy, (u, h)))
            sends.append((core_copy, (u, 0)))
        for u in (0, 1, 4, 2, 5):
            sends.append((core_copy, (u, 1)))

    def both(a, b):
        def run():
            only(first, *a)()
            only(second, *b)()

        return run

    only(second, (make_bias, 1), (o_step1,), (w_p1,), (o_step2,), (w_a, 1), (o_step3,), (w_b, 1), (spread2, 0))()
    block(0, both([(w_p1,)], [(w_a, 2)]), both([(w_a, 1), (permute, 1)], [(w_b, 2), (spread2, 1), (spread2, 4)]))
    block(1, both([(w_b, 1)], [(w_a, 3)]), both([(w_a, 2), (o_step1,)], [(w_b, 3), (spread2, 2), (spread2, 5)]))
    only(first, (w_b, 2), (o_step2,), (spread2, 0), (spread2, 1), (spread2, 4), (w_a, 3), (spread2, 2), (spread2, 5), (w_b, 3), (o_step3,))()
    del pending[:]
    remake()
    w_last()
    for u in (3, 6, 7):
        spread2(u)
    local["mw"].wait()
    local["sm"].wait()
    for u in range(8):
        spread3(u)

    for m in range(2):
        @pl.when(first)
        def _():
            for q in range(4):
                att_copy(m, q).wait_recv()
            add_projected(m, ar, oo, x2h)

        @pl.when(second)
        def _():
            for q in away[m]:
                home_copy(m, q).wait_recv()

        merge(m)

    for make, args in sends:
        make(*args).wait_send()

    @pl.when(second)
    def _():
        for m in range(2):
            for q in away[m]:
                live_copy(m, q).wait_send()
                halo(m, q, True).wait_send()
                home_copy(m, q).wait_send()


def body(fields, live_cells, norm_gain, q_weight, k_weight, v_weight, o_weight, merge_gain, merge_weight):
    perm, share, phase, cols, rows = tables()
    anywhere = pl.BlockSpec(memory_space=pltpu.HBM)
    vmem = pl.BlockSpec(memory_space=pltpu.VMEM)
    dma = pltpu.SemaphoreType.DMA
    out = pl.pallas_call(
        kernel,
        out_shape=jax.ShapeDtypeStruct((2, 18, 4, 1024), BF16),
        in_specs=[anywhere, vmem, vmem, anywhere, anywhere, anywhere, anywhere, vmem, anywhere]
        + [anywhere] * 4 + [vmem],
        out_specs=vmem,
        scratch_shapes=[
            pltpu.VMEM((2, QT, 4, D), BF16),
            pltpu.VMEM((4 * QT, D), BF16),
            pltpu.VMEM((2, NT, D), BF16),
            pltpu.VMEM((2, NT, D), BF16),
            pltpu.VMEM((2, NT, D), BF16),
            pltpu.VMEM((2, NT, DH), BF16),
            pltpu.VMEM((2, NT, DH), BF16),
            pltpu.VMEM((NT, D), BF16),
            pltpu.VMEM((NT, 3 * DH), BF16),
            pltpu.VMEM((D, 3 * DH), BF16),
            pltpu.VMEM((DH, D), BF16),
            pltpu.VMEM((DH, D), BF16),
            pltpu.VMEM((2, 8, 256, D), BF16),
            pltpu.VMEM((NT, 4 * QT), BF16),
            pltpu.VMEM((WT, WT), BF16),
            pltpu.VMEM((4 * QP, NT), BF16),
            pltpu.VMEM((4, 128, WT), BF16),
            pltpu.VMEM((2, WT, WT), F32),
            pltpu.VMEM((8, 128), F32),
            pltpu.VMEM((2, 4, 8, 128), F32),
            pltpu.VMEM((4, QP, D), F32),
            pltpu.VMEM((4, QP, D), BF16),
            dma((11,)),
            dma((2, 4)), dma((2, 4)), dma((2, 4)), dma((2, 4)), dma((2, 4)), dma((2, 4)),
            dma((2, 4)), dma((2, 4)), dma((8,)), dma((8,)), dma((2, 2, 4)), dma((2, 2, 4)), dma((1,)), dma((1,)),
            dma((8, 2)), dma((8, 2)), dma((8, 2)), dma((8, 2)),
        ],
        compiler_params=pltpu.CompilerParams(
            collective_id=0, has_side_effects=True, vmem_limit_bytes=52 * 2**20
        ),
    )(
        fields.transpose(0, 2, 3, 1, 4).reshape(2, QT, 4, D),
        live_cells,
        norm_gain,
        q_weight[0],
        k_weight[0],
        v_weight[0],
        o_weight[0],
        merge_gain.reshape(4, 1, D),
        merge_weight,
        jnp.asarray(perm, BF16),
        jnp.asarray(share, BF16),
        jnp.asarray(phase, BF16),
        jnp.asarray(cols, BF16),
        jnp.asarray(rows, F32),
    )
    return out.reshape(2, 3, 6, 4, D).transpose(0, 3, 1, 2, 4)


def solution(mesh):
    placed = (
        P(None, None, "lat", "lon", None),
        P("lat", "lon"),
        P("section", None),
        P("section", None, None),
        P("section", None, None),
        P("section", None, None),
        P("section", None, None),
        P(),
        P("lat", "section"),
    )
    return jax.shard_map(
        body, mesh=mesh, in_specs=placed, out_specs=P(None, None, "lat", "lon", "section"), check_vma=False
    )
```

```python
import jax
import jax.numpy as jnp
import numpy as np
from jax import lax
from jax.experimental import pallas as pl
from jax.experimental.pallas import tpu as pltpu
from jax.sharding import PartitionSpec as P

MESH = pl.DeviceIdType.MESH
F32 = jnp.float32
BF16 = jnp.bfloat16
QT = 72
QP = 80
NT = 4 * QP
HP = 40
WT = 4 * HP
D = 1024
DH = 512


def tables():
    perm = np.zeros((NT, 4 * QT), np.float32)
    share = np.zeros((WT, WT), np.float32)
    phase = np.zeros((4 * QP, NT), np.float32)
    cols = np.zeros((4, 128, WT), np.float32)
    rows = np.zeros((4, 8, WT), np.float32)
    where = {}
    for q in range(4):
        for t in range(QT):
            lev, r, c = t // 18, 3 * (q // 2) + t % 18 // 6, 6 * (q % 2) + t % 6
            where[lev, r, c] = q * QP + lev // 2 * HP + t % 36
            perm[where[lev, r, c], (r * 12 + c) * 4 + lev] = 1
            cols[q, c, q * HP + t % 36] = 1
            rows[q, r, q * HP + t % 36] = 1
    for a in range(WT):
        for b in range(WT):
            if a % HP < 36 and b % HP < 36:
                share[a, b] = 2 if a // (2 * HP) == b // (2 * HP) else 1
    share[np.arange(WT), np.arange(WT)] = 3
    for k in range(4):
        for lev in range(4):
            for a in range(3):
                for b in range(6):
                    phase[k * QP + (a * 6 + b) * 4 + lev, where[lev, 2 * a + k % 2, 2 * b + k // 2]] = 1
    return perm, share, phase, cols, rows


def kernel(
    x_ref, live_ref, ng_ref, q_ref, k_ref, v_ref, o_ref, mg_ref, mw_ref,
    pm_ref, em_ref, sm_ref, cs_ref, rs_ref,
    out_ref,
    xin, xp, sx, xs, x2h, ar, attb, nrm, qkv, wqkv, ow, oo, wm, pm, em, sm, cs, bias, lvown, lvs, jb, nb,
    lsem, asend, arecv, hsend, hrecv, gsend, grecv, lsend, lrecv, osend, orecv, zsend, zrecv, xsend, xrecv,
    ysend, yrecv, csend, crecv,
):
    i = lax.axis_index("lat")
    j = lax.axis_index("lon")
    s = lax.axis_index("section")
    z = lax.rem(i, 8)
    xl = lax.div(i, 8)
    y = lax.div(j, 2)
    c = lax.rem(j, 2)
    first = s == 0
    second = s == 1
    sign = 2 * s - 1

    def dev(di, dj, sec):
        return (lax.rem(i + di + 16, 16), lax.rem(j + dj + 8, 8), sec)

    def zdev(d):
        return (i - z + lax.rem(z + d + 8, 8), j, s)

    xdev = (lax.rem(i + 8, 16), j, s)
    cdev = (i, j + 1 - 2 * c, s)

    def rc(src, dst, send, recv, device):
        return pltpu.make_async_remote_copy(
            src_ref=src, dst_ref=dst, send_sem=send, recv_sem=recv, device_id=device, device_id_type=MESH
        )

    greet = [dev(0, 1, s), dev(0, -1, s), dev(1, 0, s), dev(-1, 0, s), dev(1, 1, s), dev(-1, -1, s)]
    greet += [dev(0, 2, s), dev(0, -2, s), dev(0, 4, s), zdev(1), zdev(-1), xdev]
    other = 1 - s
    greet += [dev(0, 0, other), dev(0, 1, other), dev(0, -1, other), dev(1, 0, other), dev(-1, 0, other)]
    greet += [dev(1, 1, other), dev(-1, -1, other)]
    barrier = pltpu.get_barrier_semaphore()
    for d in greet:
        pl.semaphore_signal(barrier, inc=1, device_id=d, device_id_type=MESH)

    local = {}
    plan = [
        ("x0", x_ref.at[0], xin.at[0]), ("pm", pm_ref, pm), ("x1", x_ref.at[1], xin.at[1]),
        ("cs", cs_ref, cs), ("em", em_ref, em),
        ("q", q_ref, wqkv.at[:, 0:512]), ("k", k_ref, wqkv.at[:, 512:1024]), ("v", v_ref, wqkv.at[:, 1024:1536]),
        ("o", o_ref, ow), ("mw", mw_ref, wm.at[xl, z]), ("sm", sm_ref, sm),
    ]
    for n, (name, src, dst) in enumerate(plan):
        local[name] = pltpu.make_async_copy(src, dst, lsem.at[n])
        local[name].start()

    pl.semaphore_wait(barrier, len(greet))

    def oat(ref, piece):
        return ref.at[pl.ds(pl.multiple_of(piece * 64, 64), 64)]

    def piece_at(dj):
        return lax.rem(j + dj + 8, 8)

    o_from = (2, -2, 4)
    sends = []

    def launch(make, *args):
        make(*args).start()
        sends.append((make, args))

    def o_cross():
        return rc(oat(o_ref, j), oat(oo, j), osend.at[0], orecv.at[0], dev(0, 0, other))

    def o_side(n):
        return rc(oat(oo, j), oat(oo, j), osend.at[1 + n], orecv.at[1 + n], dev(0, -o_from[n], s))

    def o_core(n):
        p = oat(oo, piece_at(((0,) + o_from)[n]))
        return rc(p, p, osend.at[4 + n], orecv.at[4 + n], cdev)

    launch(o_cross)

    def o_step1():
        o_cross().wait_recv()
        for n in range(3):
            launch(o_side, n)
        launch(o_core, 0)

    def o_step2():
        for n, dj in enumerate(o_from):
            p = oat(oo, piece_at(dj))
            rc(p, p, osend.at[1 + n], orecv.at[1 + n], dev(0, dj, s)).wait_recv()
            launch(o_core, 1 + n)

    def o_step3():
        for n, dj in enumerate((0,) + o_from):
            p = oat(oo, lax.rem(j + 1 - 2 * c + dj + 8, 8))
            rc(p, p, osend.at[4 + n], orecv.at[4 + n], cdev).wait_recv()

    e = lax.rem(y, 2)
    cls = 2 * e + c
    ocls = 2 * (1 - e) + c

    def rowsof(k, half=None):
        if half is None:
            return pl.ds(pl.multiple_of(k * 64, 64), 64)
        return pl.ds(pl.multiple_of(k * 64 + half * 32, 32), 32)

    def zat(d):
        return lax.rem(z + d + 8, 8)

    def lane_of(chain):
        return xl if chain == 0 else 1 - xl

    def hop_src(chain, way, t):
        d = -way * (t - 1)
        if chain == 0 and t == 1:
            return mw_ref.at[rowsof(cls)]
        return wm.at[lane_of(chain), zat(d), rowsof(cls)]

    def hop_copy(chain, way, t):
        w = 0 if way == 1 else 1
        dst = wm.at[lane_of(chain), zat(-way * (t - 1)), rowsof(cls)]
        return rc(hop_src(chain, way, t), dst, zsend.at[chain, w, t - 1], zrecv.at[chain, w, t - 1], zdev(way))

    def hop(chain, way, t):
        launch(hop_copy, chain, way, t)

    def hop_wait(chain, way, t):
        w = 0 if way == 1 else 1
        dst = wm.at[lane_of(chain), zat(-way * t), rowsof(cls)]
        rc(dst, dst, zsend.at[chain, w, t - 1], zrecv.at[chain, w, t - 1], zdev(way)).wait_recv()

    units = (0, -1, -2, -3, 1, 2, 3, 4)

    def block_at(u, rows):
        if u == 0:
            return wm.at[1 - xl, z, rows]
        return wm.at[:, zat(units[u]), rows]

    def side_copy(u, h):
        ref = block_at(u, rowsof(cls, h))
        return rc(ref, ref, ysend.at[u, h], yrecv.at[u, h], dev(0, 2 - 4 * h, s))

    def core_copy(u, n):
        ref = block_at(u, rowsof(ocls if n else cls))
        return rc(ref, ref, csend.at[u, n], crecv.at[u, n], cdev)

    def spread(u):
        for h in range(2):
            launch(side_copy, u, h)
        launch(core_copy, u, 0)

    def spread2(u):
        for h, dy in ((0, -2), (1, 2)):
            ref = block_at(u, rowsof(ocls, h))
            rc(ref, ref, ysend.at[u, h], yrecv.at[u, h], dev(0, dy, s)).wait_recv()
        launch(core_copy, u, 1)

    def spread3(u):
        for n, k in ((0, 2 * e + 1 - c), (1, 2 * (1 - e) + 1 - c)):
            ref = block_at(u, rowsof(k))
            rc(ref, ref, csend.at[u, n], crecv.at[u, n], cdev).wait_recv()

    def pair_copy():
        return rc(mw_ref.at[rowsof(cls)], wm.at[xl, z, rowsof(cls)], xsend.at[0], xrecv.at[0], xdev)

    def w_p0():
        launch(pair_copy)
        hop(0, 1, 1)
        hop(0, -1, 1)

    def w_p1():
        ref = wm.at[1 - xl, z, rowsof(cls)]
        rc(ref, ref, xsend.at[0], xrecv.at[0], xdev).wait_recv()
        hop(1, 1, 1)
        hop(1, -1, 1)
        spread(0)

    def w_a(t):
        for way in (1, -1):
            hop_wait(0, way, t)
            if t < 3 or way == 1:
                hop(0, way, t + 1)

    def w_b(t):
        for way in (1, -1):
            hop_wait(1, way, t)
            if t < 3 or way == -1:
                hop(1, way, t + 1)
        spread(t)
        spread(3 + t)

    def w_last():
        hop_wait(0, 1, 4)
        hop_wait(1, -1, 4)
        spread(7)

    def off(m, q):
        return (1 - q // 2, 1 - q % 2) if m == 0 else (-(q // 2), -(q % 2))

    own = (3, 0)
    away = ((0, 1, 2), (1, 2, 3))

    def permute(m):
        local[f"x{m}"].wait()
        for g in range(QT):
            xp[pl.ds(g * 4, 4), :] = xin[m, g]
        if m == 0:
            local["pm"].wait()

        def step(n, carry):
            cols = pl.ds(pl.multiple_of(n * 256, 256), 256)
            got = jnp.dot(pm[...], xp[:, cols], preferred_element_type=F32).astype(BF16)
            sx[m, :, cols] = got

            @pl.when(first)
            def _():
                xs[m, :, cols] = got

            @pl.when(second)
            def _():
                xs[m, pl.ds(own[m] * QP, QP), cols] = got[own[m] * QP : own[m] * QP + QP, :]

            return carry

        lax.fori_loop(0, 4, step, 0, unroll=True)

    def slot(ref, m, q):
        return ref.at[m, pl.ds(q * QP, QP)]

    def halo(m, q, start):
        up, side = off(m, q)
        d = dev(-up, -side, s) if start else dev(up, side, s)
        return rc(slot(sx, m, q), slot(xs, m, q), hsend.at[m, q], hrecv.at[m, q], d)

    def live_copy(m, q):
        up, side = off(m, q)
        return rc(lvown, lvs.at[m, q], lsend.at[m, q], lrecv.at[m, q], dev(-up, -side, s))

    def att_copy(m, q, h):
        up, side = off(m, q)
        rows, cols = pl.ds(q * QP, QP), pl.ds(h * 256, 256)
        return rc(
            attb.at[m, rows, cols], ar.at[m, rows, cols], asend.at[m, q, h], arecv.at[m, q, h],
            dev(sign * up, sign * side, other),
        )

    def home_copy(m, q):
        up, side = off(m, q)
        return rc(slot(xs, m, q), slot(x2h, m, q), gsend.at[m, q], grecv.at[m, q], dev(up, side, s))

    def add_projected(m, src, weight, dst):
        def step(n, carry):
            cols = pl.ds(pl.multiple_of(n * 256, 256), 256)
            got = jnp.dot(src[m], weight[:, cols], preferred_element_type=F32)
            dst[m, :, cols] = (xs[m, :, cols].astype(F32) + got).astype(BF16)
            return carry

        lax.fori_loop(0, 4, step, 0, unroll=True)

    def make_bias(m):
        alive = jnp.zeros((1, WT), F32)
        for q in range(4):
            got = jnp.dot(lvs[m, q].astype(BF16), cs[q], preferred_element_type=F32)
            alive += jnp.sum(got * rs_ref[q], axis=0, keepdims=True)
        cut = jnp.where(jnp.logical_and(second, i == (15 if m == 0 else 0)), 1.5, 0.5)
        code = em[...].astype(F32)
        ok = jnp.logical_or(jnp.logical_and(code > cut, alive > 0.5), code > 2.5)
        bias[m] = jnp.where(ok, 0.0, -1e30)

    def attend(m, hook):
        gain = ng_ref[...].astype(F32)
        for n in range(8):
            v = xs[m, n * HP : n * HP + HP, :].astype(F32)
            v = v - jnp.mean(v, axis=-1, keepdims=True)
            var = jnp.mean(v * v, axis=-1, keepdims=True)
            row = n % 2 * WT + n // 2 * HP
            nrm[row : row + HP, :] = (v * lax.rsqrt(var + 1e-05) * gain).astype(BF16)
        if m == 0:
            for name in "qkv":
                local[name].wait()

        def project(n, carry):
            cols = pl.ds(pl.multiple_of(n * 512, 512), 512)
            got = jnp.dot(nrm[...], wqkv[:, cols], preferred_element_type=F32)
            qkv[:, cols] = (got * jnp.where(n < 1, 0.125, 1.0)).astype(BF16)
            return carry

        lax.fori_loop(0, 3, project, 0, unroll=True)
        hook()
        low = lax.broadcasted_iota(jnp.int32, (WT, 128), 1) < 64
        bm = m * s

        def heads(n, carry):
            base = pl.multiple_of(n * 128, 128)
            for w in range(2):
                rows = pl.ds(w * WT, WT)
                qp = qkv[rows, pl.ds(base, 128)]
                kp = qkv[rows, pl.ds(base + 512, 128)]
                vp = qkv[rows, pl.ds(base + 1024, 128)]
                outs = []
                for mask in (low, jnp.logical_not(low)):
                    qm = jnp.where(mask, qp, jnp.zeros_like(qp))
                    sc = lax.dot_general(qm, kp, (((1,), (1,)), ((), ())), preferred_element_type=F32) + bias[bm]
                    ex = jnp.exp(sc - jnp.max(sc, axis=-1, keepdims=True))
                    total = jnp.sum(ex, axis=-1, keepdims=True)
                    got = jnp.dot(ex.astype(BF16), vp, preferred_element_type=F32)
                    outs.append(got / total)
                both = jnp.where(low, outs[0], outs[1]).astype(BF16)
                for q in range(4):
                    attb[m, pl.ds(q * QP + w * HP, HP), pl.ds(base, 128)] = both[q * HP : q * HP + HP, :]
            return carry

        for h in range(2):
            lax.fori_loop(2 * h, 2 * h + 2, heads, 0, unroll=True)
            for q in range(4):
                launch(att_copy, m, q, h)

    def block(m, middle, after):
        @pl.when(second)
        def _():
            for q in away[m]:
                halo(m, q, False).wait_recv()
            for q in range(4):
                for h in range(2):
                    att_copy(m, q, h).wait_recv()
            add_projected(m, ar, oo, xs)

        attend(m, middle)
        after()
        if m == 0:
            local["o"].wait()
        add_projected(m, attb, ow, xs)

        @pl.when(second)
        def _():
            for q in away[m]:
                home_copy(m, q).start()
            x2h[m, pl.ds(own[m] * QP, QP), :] = xs[m, pl.ds(own[m] * QP, QP), :]

    def prepare(m):
        def gather(k, carry):
            rows = pl.ds(pl.multiple_of(k * QP, QP), QP)
            jb[k] = jnp.dot(sm[rows, :], x2h[m], preferred_element_type=F32)
            return carry

        lax.fori_loop(0, 4, gather, 0, unroll=True)

        def ln(n, carry):
            rows = pl.ds(pl.multiple_of(n * 16, 16), 16)
            parts = [jb[k, rows, :] for k in range(4)]
            mean = sum(jnp.sum(p, axis=-1, keepdims=True) for p in parts) * (1.0 / 4096)
            parts = [p - mean for p in parts]
            var = sum(jnp.sum(p * p, axis=-1, keepdims=True) for p in parts) * (1.0 / 4096)
            scale = lax.rsqrt(var + 1e-05)
            for k in range(4):
                nb[k, pl.ds(m * QP + n * 16, 16), :] = (parts[k] * scale * mg_ref[k]).astype(BF16)
            return carry

        lax.fori_loop(0, 5, ln, 0, unroll=True)

    def project_merged():
        def out(n, carry):
            cols = pl.ds(pl.multiple_of(n * 256, 256), 256)
            acc = jnp.zeros((2 * QP, 256), F32)
            for k in range(4):
                w = wm[k // 2, pl.ds(4 * (k % 2), 4), :, cols].reshape(1024, 256)
                acc += jnp.dot(nb[k], w, preferred_element_type=F32)
            for m in range(2):
                for g in range(18):
                    row = m * QP + g * 4
                    out_ref[m, g, :, cols] = acc[row : row + 4].astype(BF16)
            return carry

        lax.fori_loop(0, 4, out, 0, unroll=True)

    lvown[...] = jnp.zeros_like(lvown)
    lvown[0:6, 0:12] = live_ref[...].astype(F32)

    @pl.when(first)
    def _():
        w_p0()
        for m in range(2):
            for q in away[m]:
                lvs[m, q] = lvown[...]

    for m in range(2):
        lvs[m, own[m]] = lvown[...]

    @pl.when(second)
    def _():
        for m in range(2):
            for q in away[m]:
                live_copy(m, q).start()

    permute(0)

    @pl.when(second)
    def _():
        for q in away[0]:
            halo(0, q, True).start()
        permute(1)
        for q in away[1]:
            halo(1, q, True).start()
        w_p0()
        for m in range(2):
            for q in away[m]:
                live_copy(m, q).wait_recv()

    del sends[1:]
    local["cs"].wait()
    local["em"].wait()
    make_bias(0)

    def only(which, *steps):
        def run():
            mark = len(sends)

            @pl.when(which)
            def _():
                for f, *args in steps:
                    f(*args)

            pending.extend(sends[mark:])
            del sends[mark:]

        return run

    pending = []

    def remake():
        sends.append((pair_copy, ()))
        for way in (1, -1):
            for chain in range(2):
                for n in range(1, 5 if way == 1 - 2 * chain else 4):
                    sends.append((hop_copy, (chain, way, n)))
        for n in range(3):
            sends.append((o_side, (n,)))
        for n in range(4):
            sends.append((o_core, (n,)))
        for u in range(8):
            for n in range(2):
                sends.append((side_copy, (u, n)))
                sends.append((core_copy, (u, n)))

    def both(a, b):
        def run():
            only(first, *a)()
            only(second, *b)()

        return run

    only(second, (make_bias, 1), (o_step1,), (w_p1,), (o_step2,), (w_a, 1), (o_step3,), (w_b, 1), (spread2, 0))()
    block(0, both([(w_p1,)], [(w_a, 2)]), both([(w_a, 1), (permute, 1)], [(w_b, 2), (spread2, 1), (spread2, 4)]))
    block(1, both([(w_b, 1)], [(w_a, 3)]), both([(w_a, 2), (o_step1,)], [(w_b, 3), (spread2, 2), (spread2, 5)]))
    only(first, (w_b, 2), (o_step2,), (spread2, 0), (spread2, 1), (spread2, 4), (w_a, 3), (spread2, 2), (spread2, 5), (w_b, 3), (o_step3,))()
    def arrive(m):
        @pl.when(first)
        def _():
            for q in range(4):
                for h in range(2):
                    att_copy(m, q, h).wait_recv()
            add_projected(m, ar, oo, x2h)

        @pl.when(second)
        def _():
            for q in away[m]:
                home_copy(m, q).wait_recv()

        prepare(m)

    local["sm"].wait()
    last = [(w_last,), (spread2, 3), (spread2, 6), (spread2, 7)]
    only(first, *last)()
    arrive(0)
    only(second, *last)()
    del pending[:]
    remake()
    arrive(1)
    local["mw"].wait()
    for u in range(8):
        spread3(u)
    project_merged()
    for make, args in sends:
        make(*args).wait_send()

    @pl.when(second)
    def _():
        for m in range(2):
            for q in away[m]:
                live_copy(m, q).wait_send()
                halo(m, q, True).wait_send()
                home_copy(m, q).wait_send()


def body(fields, live_cells, norm_gain, q_weight, k_weight, v_weight, o_weight, merge_gain, merge_weight):
    perm, share, phase, cols, rows = tables()
    anywhere = pl.BlockSpec(memory_space=pltpu.HBM)
    vmem = pl.BlockSpec(memory_space=pltpu.VMEM)
    dma = pltpu.SemaphoreType.DMA
    out = pl.pallas_call(
        kernel,
        out_shape=jax.ShapeDtypeStruct((2, 18, 4, 1024), BF16),
        in_specs=[anywhere, vmem, vmem, anywhere, anywhere, anywhere, anywhere, vmem, anywhere]
        + [anywhere] * 4 + [vmem],
        out_specs=vmem,
        scratch_shapes=[
            pltpu.VMEM((2, QT, 4, D), BF16),
            pltpu.VMEM((4 * QT, D), BF16),
            pltpu.VMEM((2, NT, D), BF16),
            pltpu.VMEM((2, NT, D), BF16),
            pltpu.VMEM((2, NT, D), BF16),
            pltpu.VMEM((2, NT, DH), BF16),
            pltpu.VMEM((2, NT, DH), BF16),
            pltpu.VMEM((NT, D), BF16),
            pltpu.VMEM((NT, 3 * DH), BF16),
            pltpu.VMEM((D, 3 * DH), BF16),
            pltpu.VMEM((DH, D), BF16),
            pltpu.VMEM((DH, D), BF16),
            pltpu.VMEM((2, 8, 256, D), BF16),
            pltpu.VMEM((NT, 4 * QT), BF16),
            pltpu.VMEM((WT, WT), BF16),
            pltpu.VMEM((4 * QP, NT), BF16),
            pltpu.VMEM((4, 128, WT), BF16),
            pltpu.VMEM((2, WT, WT), F32),
            pltpu.VMEM((8, 128), F32),
            pltpu.VMEM((2, 4, 8, 128), F32),
            pltpu.VMEM((4, QP, D), F32),
            pltpu.VMEM((4, 2 * QP, D), BF16),
            dma((11,)),
            dma((2, 4, 2)), dma((2, 4, 2)), dma((2, 4)), dma((2, 4)), dma((2, 4)), dma((2, 4)),
            dma((2, 4)), dma((2, 4)), dma((8,)), dma((8,)), dma((2, 2, 4)), dma((2, 2, 4)), dma((1,)), dma((1,)),
            dma((8, 2)), dma((8, 2)), dma((8, 2)), dma((8, 2)),
        ],
        compiler_params=pltpu.CompilerParams(
            collective_id=0, has_side_effects=True, vmem_limit_bytes=63 * 2**20
        ),
    )(
        fields.transpose(0, 2, 3, 1, 4).reshape(2, QT, 4, D),
        live_cells,
        norm_gain,
        q_weight[0],
        k_weight[0],
        v_weight[0],
        o_weight[0],
        merge_gain.reshape(4, 1, D),
        merge_weight,
        jnp.asarray(perm, BF16),
        jnp.asarray(share, BF16),
        jnp.asarray(phase, BF16),
        jnp.asarray(cols, BF16),
        jnp.asarray(rows, F32),
    )
    return out.reshape(2, 3, 6, 4, D).transpose(0, 3, 1, 2, 4)


def solution(mesh):
    placed = (
        P(None, None, "lat", "lon", None),
        P("lat", "lon"),
        P("section", None),
        P("section", None, None),
        P("section", None, None),
        P("section", None, None),
        P("section", None, None),
        P(),
        P("lat", "section"),
    )
    return jax.shard_map(
        body, mesh=mesh, in_specs=placed, out_specs=P(None, None, "lat", "lon", "section"), check_vma=False
    )
```

```python
import jax
import jax.numpy as jnp
import numpy as np
from jax import lax
from jax.experimental import pallas as pl
from jax.experimental.pallas import tpu as pltpu
from jax.sharding import PartitionSpec as P

MESH = pl.DeviceIdType.MESH
F32 = jnp.float32
BF16 = jnp.bfloat16
QT = 72
QP = 80
NT = 4 * QP
HP = 40
WT = 4 * HP
D = 1024
DH = 512


def tables():
    perm = np.zeros((NT, 4 * QT), np.float32)
    share = np.zeros((WT, WT), np.float32)
    phase = np.zeros((4 * QP, NT), np.float32)
    cols = np.zeros((4, 128, WT), np.float32)
    rows = np.zeros((4, 8, WT), np.float32)
    where = {}
    for q in range(4):
        for t in range(QT):
            lev, r, c = t // 18, 3 * (q // 2) + t % 18 // 6, 6 * (q % 2) + t % 6
            where[lev, r, c] = q * QP + lev // 2 * HP + t % 36
            perm[where[lev, r, c], (r * 12 + c) * 4 + lev] = 1
            cols[q, c, q * HP + t % 36] = 1
            rows[q, r, q * HP + t % 36] = 1
    for a in range(WT):
        for b in range(WT):
            if a % HP < 36 and b % HP < 36:
                share[a, b] = 2 if a // (2 * HP) == b // (2 * HP) else 1
    share[np.arange(WT), np.arange(WT)] = 3
    for k in range(4):
        for lev in range(4):
            for a in range(3):
                for b in range(6):
                    phase[k * QP + (a * 6 + b) * 4 + lev, where[lev, 2 * a + k % 2, 2 * b + k // 2]] = 1
    return perm, share, phase, cols, rows


def kernel(
    x_ref, live_ref, ng_ref, q_ref, k_ref, v_ref, o_ref, mg_ref, mw_ref,
    pm_ref, em_ref, sm_ref, cs_ref, rs_ref,
    out_ref,
    xin, xp, sx, xs, x2h, ar, attb, nrm, qkv, wqkv, ow, oo, wm, pm, em, sm, cs, bias, lvown, lvs, jb, nb,
    lsem, asend, arecv, hsend, hrecv, gsend, grecv, lsend, lrecv, osend, orecv, zsend, zrecv, xsend, xrecv,
    ysend, yrecv, csend, crecv,
):
    i = lax.axis_index("lat")
    j = lax.axis_index("lon")
    s = lax.axis_index("section")
    z = lax.rem(i, 8)
    xl = lax.div(i, 8)
    y = lax.div(j, 2)
    c = lax.rem(j, 2)
    first = s == 0
    second = s == 1
    sign = 2 * s - 1

    def dev(di, dj, sec):
        return (lax.rem(i + di + 16, 16), lax.rem(j + dj + 8, 8), sec)

    def zdev(d):
        return (i - z + lax.rem(z + d + 8, 8), j, s)

    xdev = (lax.rem(i + 8, 16), j, s)
    cdev = (i, j + 1 - 2 * c, s)

    def rc(src, dst, send, recv, device):
        return pltpu.make_async_remote_copy(
            src_ref=src, dst_ref=dst, send_sem=send, recv_sem=recv, device_id=device, device_id_type=MESH
        )

    greet = [dev(0, 1, s), dev(0, -1, s), dev(1, 0, s), dev(-1, 0, s), dev(1, 1, s), dev(-1, -1, s)]
    greet += [dev(0, 2, s), dev(0, -2, s), dev(0, 4, s), zdev(1), zdev(-1), xdev]
    other = 1 - s
    greet += [dev(0, 0, other), dev(0, 1, other), dev(0, -1, other), dev(1, 0, other), dev(-1, 0, other)]
    greet += [dev(1, 1, other), dev(-1, -1, other)]
    barrier = pltpu.get_barrier_semaphore()
    for d in greet:
        pl.semaphore_signal(barrier, inc=1, device_id=d, device_id_type=MESH)

    local = {}
    plan = [
        ("x0", x_ref.at[0], xin.at[0]), ("pm", pm_ref, pm), ("x1", x_ref.at[1], xin.at[1]),
        ("cs", cs_ref, cs), ("em", em_ref, em),
        ("q", q_ref, wqkv.at[:, 0:512]), ("k", k_ref, wqkv.at[:, 512:1024]), ("v", v_ref, wqkv.at[:, 1024:1536]),
        ("o", o_ref, ow), ("mw", mw_ref, wm.at[xl, z]), ("sm", sm_ref, sm),
    ]
    for n, (name, src, dst) in enumerate(plan):
        local[name] = pltpu.make_async_copy(src, dst, lsem.at[n])
        local[name].start()

    pl.semaphore_wait(barrier, len(greet))

    def oat(ref, piece):
        return ref.at[pl.ds(pl.multiple_of(piece * 64, 64), 64)]

    def piece_at(dj):
        return lax.rem(j + dj + 8, 8)

    o_from = (2, -2, 4)
    sends = []

    def launch(make, *args):
        make(*args).start()
        sends.append((make, args))

    def o_cross():
        return rc(oat(o_ref, j), oat(oo, j), osend.at[0], orecv.at[0], dev(0, 0, other))

    def o_side(n):
        return rc(oat(oo, j), oat(oo, j), osend.at[1 + n], orecv.at[1 + n], dev(0, -o_from[n], s))

    def o_core(n):
        p = oat(oo, piece_at(((0,) + o_from)[n]))
        return rc(p, p, osend.at[4 + n], orecv.at[4 + n], cdev)

    launch(o_cross)

    def o_step1():
        o_cross().wait_recv()
        for n in range(3):
            launch(o_side, n)
        launch(o_core, 0)

    def o_step2():
        for n, dj in enumerate(o_from):
            p = oat(oo, piece_at(dj))
            rc(p, p, osend.at[1 + n], orecv.at[1 + n], dev(0, dj, s)).wait_recv()
            launch(o_core, 1 + n)

    def o_step3():
        for n, dj in enumerate((0,) + o_from):
            p = oat(oo, lax.rem(j + 1 - 2 * c + dj + 8, 8))
            rc(p, p, osend.at[4 + n], orecv.at[4 + n], cdev).wait_recv()

    e = lax.rem(y, 2)
    cls = 2 * e + c
    ocls = 2 * (1 - e) + c

    def rowsof(k, half=None):
        if half is None:
            return pl.ds(pl.multiple_of(k * 64, 64), 64)
        return pl.ds(pl.multiple_of(k * 64 + half * 32, 32), 32)

    def zat(d):
        return lax.rem(z + d + 8, 8)

    def lane_of(chain):
        return xl if chain == 0 else 1 - xl

    def hop_src(chain, way, t):
        d = -way * (t - 1)
        if chain == 0 and t == 1:
            return mw_ref.at[rowsof(cls)]
        return wm.at[lane_of(chain), zat(d), rowsof(cls)]

    def hop_copy(chain, way, t):
        w = 0 if way == 1 else 1
        dst = wm.at[lane_of(chain), zat(-way * (t - 1)), rowsof(cls)]
        return rc(hop_src(chain, way, t), dst, zsend.at[chain, w, t - 1], zrecv.at[chain, w, t - 1], zdev(way))

    def hop(chain, way, t):
        launch(hop_copy, chain, way, t)

    def hop_wait(chain, way, t):
        w = 0 if way == 1 else 1
        dst = wm.at[lane_of(chain), zat(-way * t), rowsof(cls)]
        rc(dst, dst, zsend.at[chain, w, t - 1], zrecv.at[chain, w, t - 1], zdev(way)).wait_recv()

    units = (0, -1, -2, -3, 1, 2, 3, 4)

    def block_at(u, rows):
        if u == 0:
            return wm.at[1 - xl, z, rows]
        return wm.at[:, zat(units[u]), rows]

    def side_copy(u, h):
        ref = block_at(u, rowsof(cls, h))
        return rc(ref, ref, ysend.at[u, h], yrecv.at[u, h], dev(0, 2 - 4 * h, s))

    def core_copy(u, n):
        ref = block_at(u, rowsof(ocls if n else cls))
        return rc(ref, ref, csend.at[u, n], crecv.at[u, n], cdev)

    def spread(u):
        for h in range(2):
            launch(side_copy, u, h)
        launch(core_copy, u, 0)

    def spread2(u):
        for h, dy in ((0, -2), (1, 2)):
            ref = block_at(u, rowsof(ocls, h))
            rc(ref, ref, ysend.at[u, h], yrecv.at[u, h], dev(0, dy, s)).wait_recv()
        launch(core_copy, u, 1)

    def spread3(u):
        for n, k in ((0, 2 * e + 1 - c), (1, 2 * (1 - e) + 1 - c)):
            ref = block_at(u, rowsof(k))
            rc(ref, ref, csend.at[u, n], crecv.at[u, n], cdev).wait_recv()

    def pair_copy():
        return rc(mw_ref.at[rowsof(cls)], wm.at[xl, z, rowsof(cls)], xsend.at[0], xrecv.at[0], xdev)

    def w_p0():
        launch(pair_copy)
        hop(0, 1, 1)
        hop(0, -1, 1)

    def w_p1():
        ref = wm.at[1 - xl, z, rowsof(cls)]
        rc(ref, ref, xsend.at[0], xrecv.at[0], xdev).wait_recv()
        hop(1, 1, 1)
        hop(1, -1, 1)
        spread(0)

    def w_a(t):
        for way in (1, -1):
            hop_wait(0, way, t)
            if t < 3 or way == 1:
                hop(0, way, t + 1)

    def w_b(t):
        for way in (1, -1):
            hop_wait(1, way, t)
            if t < 3 or way == -1:
                hop(1, way, t + 1)
        spread(t)
        spread(3 + t)

    def w_last():
        hop_wait(0, 1, 4)
        hop_wait(1, -1, 4)
        spread(7)

    def off(m, q):
        return (1 - q // 2, 1 - q % 2) if m == 0 else (-(q // 2), -(q % 2))

    own = (3, 0)
    away = ((0, 1, 2), (3, 2, 1))

    def permute(m):
        local[f"x{m}"].wait()
        for g in range(QT):
            xp[pl.ds(g * 4, 4), :] = xin[m, g]
        if m == 0:
            local["pm"].wait()

        def step(n, carry):
            cols = pl.ds(pl.multiple_of(n * 256, 256), 256)
            got = jnp.dot(pm[...], xp[:, cols], preferred_element_type=F32).astype(BF16)
            sx[m, :, cols] = got

            @pl.when(first)
            def _():
                xs[m, :, cols] = got

            @pl.when(second)
            def _():
                xs[m, pl.ds(own[m] * QP, QP), cols] = got[own[m] * QP : own[m] * QP + QP, :]

            return carry

        lax.fori_loop(0, 4, step, 0, unroll=True)

    def slot(ref, m, q):
        return ref.at[m, pl.ds(q * QP, QP)]

    def halo(m, q, start):
        up, side = off(m, q)
        d = dev(-up, -side, s) if start else dev(up, side, s)
        return rc(slot(sx, m, q), slot(xs, m, q), hsend.at[m, q], hrecv.at[m, q], d)

    def live_copy(m, q):
        up, side = off(m, q)
        return rc(lvown, lvs.at[m, q], lsend.at[m, q], lrecv.at[m, q], dev(-up, -side, s))

    def att_copy(m, q, h):
        up, side = off(m, q)
        rows, cols = pl.ds(q * QP, QP), pl.ds(h * 256, 256)
        return rc(
            attb.at[m, rows, cols], ar.at[m, rows, cols], asend.at[m, q, h], arecv.at[m, q, h],
            dev(sign * up, sign * side, other),
        )

    def home_copy(m, q):
        up, side = off(m, q)
        return rc(slot(xs, m, q), slot(x2h, m, q), gsend.at[m, q], grecv.at[m, q], dev(up, side, s))

    def add_projected(m, src, weight, dst):
        def step(n, carry):
            cols = pl.ds(pl.multiple_of(n * 256, 256), 256)
            got = jnp.dot(src[m], weight[:, cols], preferred_element_type=F32)
            dst[m, :, cols] = (xs[m, :, cols].astype(F32) + got).astype(BF16)
            return carry

        lax.fori_loop(0, 4, step, 0, unroll=True)

    def make_bias(m):
        alive = jnp.zeros((1, WT), F32)
        for q in range(4):
            got = jnp.dot(lvs[m, q].astype(BF16), cs[q], preferred_element_type=F32)
            alive += jnp.sum(got * rs_ref[q], axis=0, keepdims=True)
        cut = jnp.where(jnp.logical_and(second, i == (15 if m == 0 else 0)), 1.5, 0.5)
        code = em[...].astype(F32)
        ok = jnp.logical_or(jnp.logical_and(code > cut, alive > 0.5), code > 2.5)
        bias[m] = jnp.where(ok, 0.0, -1e30)

    def attend(m, hook):
        gain = ng_ref[...].astype(F32)
        for n in range(8):
            v = xs[m, n * HP : n * HP + HP, :].astype(F32)
            v = v - jnp.mean(v, axis=-1, keepdims=True)
            var = jnp.mean(v * v, axis=-1, keepdims=True)
            row = n % 2 * WT + n // 2 * HP
            nrm[row : row + HP, :] = (v * lax.rsqrt(var + 1e-05) * gain).astype(BF16)
        if m == 0:
            for name in "qkv":
                local[name].wait()

        def project(n, carry):
            cols = pl.ds(pl.multiple_of(n * 512, 512), 512)
            got = jnp.dot(nrm[...], wqkv[:, cols], preferred_element_type=F32)
            qkv[:, cols] = (got * jnp.where(n < 1, 0.125, 1.0)).astype(BF16)
            return carry

        lax.fori_loop(0, 3, project, 0, unroll=True)
        hook()
        low = lax.broadcasted_iota(jnp.int32, (WT, 128), 1) < 64
        bm = m * s

        def heads(n, carry):
            base = pl.multiple_of(n * 128, 128)
            for w in range(2):
                rows = pl.ds(w * WT, WT)
                qp = qkv[rows, pl.ds(base, 128)]
                kp = qkv[rows, pl.ds(base + 512, 128)]
                vp = qkv[rows, pl.ds(base + 1024, 128)]
                outs = []
                for mask in (low, jnp.logical_not(low)):
                    qm = jnp.where(mask, qp, jnp.zeros_like(qp))
                    sc = lax.dot_general(qm, kp, (((1,), (1,)), ((), ())), preferred_element_type=F32) + bias[bm]
                    ex = jnp.exp(sc - jnp.max(sc, axis=-1, keepdims=True))
                    total = jnp.sum(ex, axis=-1, keepdims=True)
                    got = jnp.dot(ex.astype(BF16), vp, preferred_element_type=F32)
                    outs.append(got / total)
                both = jnp.where(low, outs[0], outs[1]).astype(BF16)
                for q in range(4):
                    attb[m, pl.ds(q * QP + w * HP, HP), pl.ds(base, 128)] = both[q * HP : q * HP + HP, :]
            return carry

        for h in range(2):
            lax.fori_loop(2 * h, 2 * h + 2, heads, 0, unroll=True)
            for q in (range(4), range(3, -1, -1))[m]:
                launch(att_copy, m, q, h)

    def block(m, middle, after):
        @pl.when(second)
        def _():
            for q in away[m]:
                halo(m, q, False).wait_recv()
            for q in range(4):
                for h in range(2):
                    att_copy(m, q, h).wait_recv()
            add_projected(m, ar, oo, xs)

        attend(m, middle)
        after()
        if m == 0:
            local["o"].wait()
        add_projected(m, attb, ow, xs)

        @pl.when(second)
        def _():
            for q in away[m]:
                home_copy(m, q).start()
            x2h[m, pl.ds(own[m] * QP, QP), :] = xs[m, pl.ds(own[m] * QP, QP), :]

    def prepare(m):
        def gather(k, carry):
            rows = pl.ds(pl.multiple_of(k * QP, QP), QP)
            jb[k] = jnp.dot(sm[rows, :], x2h[m], preferred_element_type=F32)
            return carry

        lax.fori_loop(0, 4, gather, 0, unroll=True)

        def ln(n, carry):
            rows = pl.ds(pl.multiple_of(n * 16, 16), 16)
            parts = [jb[k, rows, :] for k in range(4)]
            mean = sum(jnp.sum(p, axis=-1, keepdims=True) for p in parts) * (1.0 / 4096)
            parts = [p - mean for p in parts]
            var = sum(jnp.sum(p * p, axis=-1, keepdims=True) for p in parts) * (1.0 / 4096)
            scale = lax.rsqrt(var + 1e-05)
            for k in range(4):
                nb[k, pl.ds(m * QP + n * 16, 16), :] = (parts[k] * scale * mg_ref[k]).astype(BF16)
            return carry

        lax.fori_loop(0, 5, ln, 0, unroll=True)

    def project_merged():
        def out(n, carry):
            cols = pl.ds(pl.multiple_of(n * 256, 256), 256)
            acc = jnp.zeros((2 * QP, 256), F32)
            for k in range(4):
                w = wm[k // 2, pl.ds(4 * (k % 2), 4), :, cols].reshape(1024, 256)
                acc += jnp.dot(nb[k], w, preferred_element_type=F32)
            for m in range(2):
                for g in range(18):
                    row = m * QP + g * 4
                    out_ref[m, g, :, cols] = acc[row : row + 4].astype(BF16)
            return carry

        lax.fori_loop(0, 4, out, 0, unroll=True)

    lvown[...] = jnp.zeros_like(lvown)
    lvown[0:6, 0:12] = live_ref[...].astype(F32)

    @pl.when(first)
    def _():
        w_p0()
        for m in range(2):
            for q in away[m]:
                lvs[m, q] = lvown[...]

    for m in range(2):
        lvs[m, own[m]] = lvown[...]

    @pl.when(second)
    def _():
        for m in range(2):
            for q in away[m]:
                live_copy(m, q).start()

    permute(0)

    @pl.when(second)
    def _():
        for q in away[0]:
            halo(0, q, True).start()
        permute(1)
        for q in away[1]:
            halo(1, q, True).start()
        w_p0()
        for m in range(2):
            for q in away[m]:
                live_copy(m, q).wait_recv()

    del sends[1:]
    local["cs"].wait()
    local["em"].wait()
    make_bias(0)

    def only(which, *steps):
        def run():
            mark = len(sends)

            @pl.when(which)
            def _():
                for f, *args in steps:
                    f(*args)

            pending.extend(sends[mark:])
            del sends[mark:]

        return run

    pending = []

    def remake():
        sends.append((pair_copy, ()))
        for way in (1, -1):
            for chain in range(2):
                for n in range(1, 5 if way == 1 - 2 * chain else 4):
                    sends.append((hop_copy, (chain, way, n)))
        for n in range(3):
            sends.append((o_side, (n,)))
        for n in range(4):
            sends.append((o_core, (n,)))
        for u in range(8):
            for n in range(2):
                sends.append((side_copy, (u, n)))
                sends.append((core_copy, (u, n)))

    def both(a, b):
        def run():
            only(first, *a)()
            only(second, *b)()

        return run

    only(second, (make_bias, 1), (o_step1,), (w_p1,), (o_step2,), (w_a, 1), (o_step3,), (w_b, 1), (spread2, 0))()
    block(0, both([(w_p1,)], [(w_a, 2)]), both([(w_a, 1), (permute, 1)], [(w_b, 2), (spread2, 1), (spread2, 4)]))
    block(1, both([(w_b, 1)], [(w_a, 3)]), both([(w_a, 2), (o_step1,)], [(w_b, 3), (spread2, 2), (spread2, 5)]))
    only(first, (w_b, 2), (o_step2,), (spread2, 0), (spread2, 1), (spread2, 4), (w_a, 3), (spread2, 2), (spread2, 5), (w_b, 3), (o_step3,))()
    def arrive(m):
        @pl.when(first)
        def _():
            for q in range(4):
                for h in range(2):
                    att_copy(m, q, h).wait_recv()
            add_projected(m, ar, oo, x2h)

        @pl.when(second)
        def _():
            for q in away[m]:
                home_copy(m, q).wait_recv()

        prepare(m)

    local["sm"].wait()
    last = [(w_last,), (spread2, 3), (spread2, 6), (spread2, 7)]
    only(first, *last)()
    arrive(0)
    only(second, *last)()
    del pending[:]
    remake()
    arrive(1)
    local["mw"].wait()
    for u in range(8):
        spread3(u)
    project_merged()
    for make, args in sends:
        make(*args).wait_send()

    @pl.when(second)
    def _():
        for m in range(2):
            for q in away[m]:
                live_copy(m, q).wait_send()
                halo(m, q, True).wait_send()
                home_copy(m, q).wait_send()


def body(fields, live_cells, norm_gain, q_weight, k_weight, v_weight, o_weight, merge_gain, merge_weight):
    perm, share, phase, cols, rows = tables()
    anywhere = pl.BlockSpec(memory_space=pltpu.HBM)
    vmem = pl.BlockSpec(memory_space=pltpu.VMEM)
    dma = pltpu.SemaphoreType.DMA
    out = pl.pallas_call(
        kernel,
        out_shape=jax.ShapeDtypeStruct((2, 18, 4, 1024), BF16),
        in_specs=[anywhere, vmem, vmem, anywhere, anywhere, anywhere, anywhere, vmem, anywhere]
        + [anywhere] * 4 + [vmem],
        out_specs=vmem,
        scratch_shapes=[
            pltpu.VMEM((2, QT, 4, D), BF16),
            pltpu.VMEM((4 * QT, D), BF16),
            pltpu.VMEM((2, NT, D), BF16),
            pltpu.VMEM((2, NT, D), BF16),
            pltpu.VMEM((2, NT, D), BF16),
            pltpu.VMEM((2, NT, DH), BF16),
            pltpu.VMEM((2, NT, DH), BF16),
            pltpu.VMEM((NT, D), BF16),
            pltpu.VMEM((NT, 3 * DH), BF16),
            pltpu.VMEM((D, 3 * DH), BF16),
            pltpu.VMEM((DH, D), BF16),
            pltpu.VMEM((DH, D), BF16),
            pltpu.VMEM((2, 8, 256, D), BF16),
            pltpu.VMEM((NT, 4 * QT), BF16),
            pltpu.VMEM((WT, WT), BF16),
            pltpu.VMEM((4 * QP, NT), BF16),
            pltpu.VMEM((4, 128, WT), BF16),
            pltpu.VMEM((2, WT, WT), F32),
            pltpu.VMEM((8, 128), F32),
            pltpu.VMEM((2, 4, 8, 128), F32),
            pltpu.VMEM((4, QP, D), F32),
            pltpu.VMEM((4, 2 * QP, D), BF16),
            dma((11,)),
            dma((2, 4, 2)), dma((2, 4, 2)), dma((2, 4)), dma((2, 4)), dma((2, 4)), dma((2, 4)),
            dma((2, 4)), dma((2, 4)), dma((8,)), dma((8,)), dma((2, 2, 4)), dma((2, 2, 4)), dma((1,)), dma((1,)),
            dma((8, 2)), dma((8, 2)), dma((8, 2)), dma((8, 2)),
        ],
        compiler_params=pltpu.CompilerParams(
            collective_id=0, has_side_effects=True, vmem_limit_bytes=63 * 2**20
        ),
    )(
        fields.transpose(0, 2, 3, 1, 4).reshape(2, QT, 4, D),
        live_cells,
        norm_gain,
        q_weight[0],
        k_weight[0],
        v_weight[0],
        o_weight[0],
        merge_gain.reshape(4, 1, D),
        merge_weight,
        jnp.asarray(perm, BF16),
        jnp.asarray(share, BF16),
        jnp.asarray(phase, BF16),
        jnp.asarray(cols, BF16),
        jnp.asarray(rows, F32),
    )
    return out.reshape(2, 3, 6, 4, D).transpose(0, 3, 1, 2, 4)


def solution(mesh):
    placed = (
        P(None, None, "lat", "lon", None),
        P("lat", "lon"),
        P("section", None),
        P("section", None, None),
        P("section", None, None),
        P("section", None, None),
        P("section", None, None),
        P(),
        P("lat", "section"),
    )
    return jax.shard_map(
        body, mesh=mesh, in_specs=placed, out_specs=P(None, None, "lat", "lon", "section"), check_vma=False
    )
```
